128 devices in a mesh: wide: 32 (over y, z, core), narrow: 4 (over x).
Axes of the slice: x: 4, y: 4, z: 4, core: 2. Of those that a mesh axis runs over, the one named last changes fastest.
Arguments:
- field: bfloat16 [512, 2, 256, 1536], P('wide', None, None, 'narrow'), may hold values from -6 to 6
- table: bfloat16 [256, 1024, 1536], P('wide', None, 'narrow'), may hold values from -0.15625 to 0.15625
- inverse: bfloat16 [1024, 512, 512], P(('wide', 'narrow')), may hold values from -0.25 to 0.25
- modes: int32 [256], P('wide'), may hold values from 0 to 1023, as said below
Outputs:
- solved: float32 [1024, 2, 256, 512], P(('wide', 'narrow'))
The draws below stay inside these ranges and needn't reach their ends.
Inputs may be any that keep to these rules, and one draw needn't show every extreme that they name: `modes`: each index of wide owns 4 * 2 consecutive slots; its slot i and slot i + 4 hold a pair m and 1023 - m with m < 512; no m is held twice.
All inputs are finite; a program needn't handle non-finite values.
Results may differ from the reference program's by a relative error of at most 0.013.
Values may be sent and summed in bfloat16 or wider, within the bound.
A program may use at most 128 MiB of HBM per device.

```python
import jax
import jax.numpy as jnp
from jax import lax

L = 1024
NTH = 1536
PAIRS_DEV = 4
NR = 512
MWIN = 256
N_NARROW = 4


def draw_modes(key, part):
    key = jax.random.fold_in(key, 7)
    first, second = jax.random.split(key)
    count = MWIN // 2
    others = jax.random.permutation(first, L // 2 - 1)[:count - 1] + 1
    lows = jnp.concatenate([jnp.zeros((1,), jnp.int32), others.astype(jnp.int32)])
    lows = lows[jax.random.permutation(second, count)]
    lows = lows.reshape(-1, PAIRS_DEV)
    return jnp.concatenate([lows, L - 1 - lows], axis=1).reshape(-1).astype(jnp.int32)


def levels(stream_key, extent, cuts, least, high):
    def one(axis_at, parts):
        heights = jax.random.uniform(jax.random.fold_in(jax.random.fold_in(stream_key, 6), axis_at), (parts,), jnp.float32, least / len(cuts), high / len(cuts))
        return jnp.repeat(jnp.exp(heights), extent[axis_at] // parts).reshape((-1,) + (1,) * (len(extent) - axis_at - 1))

    loudness = one(*cuts[0])
    for cut in cuts[1:]:
        loudness = loudness * one(*cut)
    return loudness


def scatter_about(key, extent, spread, bound, shards=(), kind=jnp.bfloat16):
    values = spread * jax.random.normal(key, extent, jnp.float32)
    if shards:
        values = values * levels(key, extent, shards, -0.22, 0.18)
    return jnp.clip(values, -bound, bound).astype(kind)


def setup_inputs(seed: int = 0) -> dict:
    streams_of = jax.random.split(jax.random.key(seed), 5)
    return {
        "field": scatter_about(streams_of[0], (NR, 2, MWIN, NTH), 1.0, 6.0, ((0, 32), (3, 4))),
        "table": scatter_about(streams_of[1], (MWIN, L, NTH), NTH ** -0.5, 0.15625, ((0, 32), (2, 4))),
        "inverse": scatter_about(streams_of[2], (L, NR, NR), NR ** -0.5, 0.25, ((0, 128),)),
        "modes": draw_modes(jax.random.fold_in(streams_of[4], 71), 0),
    }


def reference(field, table, inverse, modes):
    degree = jnp.arange(L, dtype=jnp.int32)
    width_block = NTH // N_NARROW

    def per_slot(items):
        plane, row_lookup, mode = items
        filtered_entries = jnp.where(degree[:, None] >= mode, row_lookup, jnp.zeros_like(row_lookup)).astype(jnp.float32)
        values = plane.astype(jnp.float32)
        total = jnp.zeros((L, 2, NR), jnp.float32)
        for block in range(N_NARROW):
            lower = block * width_block
            upper = lower + width_block
            part = jnp.einsum("lt,rct->lcr", filtered_entries[:, lower:upper], values[:, :, lower:upper])
            part = lax.optimization_barrier(part.astype(jnp.bfloat16))
            total = total + part.astype(jnp.float32)
        return total.astype(jnp.bfloat16)

    harmonic_coefficient = lax.map(per_slot, (jnp.moveaxis(field, 2, 0), table, modes))
    harmonic_coefficient = jnp.transpose(harmonic_coefficient, (1, 2, 0, 3))

    def degree_values(items):
        matrix, coeffs = items
        return jnp.einsum("sr,cjr->cjs", matrix.astype(jnp.float32), coeffs.astype(jnp.float32))

    return lax.map(degree_values, (inverse, harmonic_coefficient))
```

```python
import functools

import jax
import jax.numpy as jnp
from jax import lax
from jax.experimental import pallas as pl
from jax.experimental.pallas import tpu as pltpu
from jax.sharding import PartitionSpec as P

MESH = pl.DeviceIdType.MESH
BF16 = jnp.bfloat16
F32 = jnp.float32

WIDE = 32
NARROW = 4
CHIPS = 16
DEG = 1024
POS = 33
ROWS = POS * 64
NCH = 4
TB = 384

PLANE = [
    (0, 1), (1, 0), (0, 3), (3, 0), (1, 1), (3, 3), (1, 3), (3, 1),
    (0, 2), (2, 0), (1, 2), (2, 1), (3, 2), (2, 3), (2, 2),
]


def transform_kernel(
    field, table, modes, inverse,
    crecv, invt,
    arecv, tabv, modv, ft, res, pbuf, brecv, csend, invv, invo, perm,
    a_send, a_recv, t_sem, b_send, b_recv, c_send, c_recv, i_sem,
):
    w = lax.axis_index("wide")
    n = lax.axis_index("narrow")
    q = w // 2
    core = w % 2
    y = q // 4
    z = q % 4
    sib = w + 1 - 2 * core

    own_table = pltpu.make_async_copy(table, tabv.at[core], t_sem.at[0])
    own_table.start()
    own_modes = pltpu.make_async_copy(modes, modv.at[core], t_sem.at[1])
    own_modes.start()
    inv_in = pltpu.make_async_copy(inverse, invv, i_sem.at[0])
    inv_in.start()
    for k in range(NCH):
        pltpu.make_async_copy(
            field.at[pl.ds(8 * (k % 2), 8), k // 2, q], arecv.at[k, q], a_recv.at[k]
        ).start()

    barrier = pltpu.get_barrier_semaphore()

    def greet(t, carry):
        pl.semaphore_signal(
            barrier, inc=1, device_id=(lax.rem(w + t, WIDE), n), device_id_type=MESH
        )
        return carry

    lax.fori_loop(1, WIDE, greet, 0)
    for d in range(1, NARROW):
        pl.semaphore_signal(
            barrier, inc=1, device_id=(w, lax.rem(n + d, NARROW)), device_id_type=MESH
        )
    pl.semaphore_wait(barrier, WIDE - 1 + NARROW - 1)

    def send_field(k):
        for dy, dz in PLANE:
            peer = lax.rem(y + dy, 4) * 4 + lax.rem(z + dz, 4)
            pltpu.make_async_remote_copy(
                src_ref=field.at[pl.ds(8 * (k % 2), 8), k // 2, peer],
                dst_ref=arecv.at[k, q],
                send_sem=a_send.at[k],
                recv_sem=a_recv.at[k],
                device_id=(peer * 2 + core, n),
                device_id_type=MESH,
            ).start()

    give_modes = pltpu.make_async_remote_copy(
        src_ref=modes, dst_ref=modv.at[core], send_sem=t_sem.at[2],
        recv_sem=t_sem.at[3], device_id=(sib, n), device_id_type=MESH,
    )
    give_modes.start()
    give_table = pltpu.make_async_remote_copy(
        src_ref=table, dst_ref=tabv.at[core], send_sem=t_sem.at[4],
        recv_sem=t_sem.at[5], device_id=(sib, n), device_id_type=MESH,
    )
    send_field(0)
    give_table.start()
    send_field(1)

    inv_in.wait()
    arrive = lax.broadcasted_iota(jnp.int32, (512, 512), 0)
    natural = (
        ((arrive // 8) % 16) * 32 + (arrive // 256) * 16 + ((arrive // 128) % 2) * 8 + arrive % 8
    )
    radius = lax.broadcasted_iota(jnp.int32, (512, 512), 1)
    perm[...] = jnp.where(radius == natural, 1.0, 0.0).astype(BF16)

    def reorder(t, carry):
        invo[t] = lax.dot_general(
            perm[...], invv[t], (((1,), (1,)), ((), ())), preferred_element_type=F32
        ).astype(BF16)
        return carry

    lax.fori_loop(0, 8, reorder, 0)
    inv_out = pltpu.make_async_copy(invo, invt, i_sem.at[1])
    inv_out.start()

    own_table.wait()
    own_modes.wait()
    give_modes.wait()
    give_table.wait()

    def transform(k):
        whole = arecv.at[k]
        pltpu.make_async_copy(whole, whole, a_recv.at[k]).wait()
        if k + 2 < NCH:
            send_field(k + 2)

        def turn(t, carry):
            block = arecv[k, pl.ds(2 * t, 2)].reshape(16, 16, TB)
            ft[:, pl.ds(pl.multiple_of(16 * t, 16), 16), :] = jnp.swapaxes(block, 0, 1)
            return carry

        lax.fori_loop(0, 8, turn, 0)

        def two_pairs(pp, carry):
            side = pp // 2
            first = 2 * (pp % 2)
            for e in range(2):
                for kind in range(2):
                    slot = first + e + 4 * kind

                    def rows(b, c2):
                        at = pl.ds(pl.multiple_of(b * 256, 256), 256)
                        res[e, kind, at, :] = lax.dot_general(
                            tabv[side, slot, at, :], ft[side * 8 + slot],
                            (((1,), (1,)), ((), ())), preferred_element_type=F32,
                        )
                        return c2

                    lax.fori_loop(0, DEG // 256, rows, 0)

            at32 = lax.broadcasted_iota(jnp.int32, (32, 128), 0)

            def part(e, kind, block):
                rows = res[e, kind, pl.ds(pl.multiple_of(block * 32, 32), 32), :]
                m = modv[side, pl.ds(first + e + 4 * kind, 1), :]
                return jnp.where(at32 + block * 32 >= m, rows, 0.0)

            def put(pos, vals):
                for t in range(NARROW):
                    both = jnp.concatenate([v[8 * t:8 * t + 8] for v in vals], axis=0)
                    pbuf[k, t, pl.ds(pl.multiple_of(pos * 64 + pp * 16, 16), 16), :] = (
                        both.astype(BF16)
                    )

            put(0, [part(e, 1, 31) for e in range(2)])
            put(32, [part(e, 0, 31) for e in range(2)])

            def fold(v, c2):
                put(v + 1, [part(e, 0, v) + part(e, 1, 30 - v) for e in range(2)])
                return c2

            lax.fori_loop(0, 31, fold, 0)
            return carry

        lax.fori_loop(0, 4, two_pairs, 0)
        for d in range(1, NARROW):
            to = lax.rem(n + d, NARROW)
            pltpu.make_async_remote_copy(
                src_ref=pbuf.at[k, to], dst_ref=brecv.at[k, d - 1],
                send_sem=b_send.at[k], recv_sem=b_recv.at[k],
                device_id=(w, to), device_id_type=MESH,
            ).start()

    def spectral(k):
        whole = brecv.at[k]
        pltpu.make_async_copy(whole, whole, b_recv.at[k]).wait()

        def modes_of(kind):
            return jnp.concatenate(
                [modv[s, 4 * kind:4 * kind + 4, :] for s in range(2)], axis=0
            )

        lo_modes, hi_modes = modes_of(0), modes_of(1)
        at = lax.broadcasted_iota(jnp.int32, (8, 8, 128), 0)

        def put(pos, v, kind, m):
            rows = pl.ds(pl.multiple_of(pos * 64, 64), 64)
            total = pbuf[k, n, rows, :].astype(F32)
            for d in range(NARROW - 1):
                total = total + brecv[k, d, rows, :].astype(F32)
            turned = jnp.swapaxes(total.reshape(8, 8, 128), 0, 1)
            kept = jnp.where(at + (v * 32 + n * 8) >= m[None], turned, 0.0)
            csend[k, 2 * v + kind] = kept.reshape(64, 128).astype(BF16)

        def low(v, carry):
            put(v + 1, v, 0, lo_modes)
            return carry

        def high(v, carry):
            put(31 - v, v, 1, hi_modes)
            return carry

        lax.fori_loop(0, WIDE, low, 0)
        lax.fori_loop(WIDE // 2, WIDE, high, 0)

        @pl.when(w >= WIDE // 2)
        def _():
            pltpu.make_async_copy(
                csend.at[k, pl.ds(2 * w, 2)], crecv.at[k, pl.ds(2 * w, 2)], c_recv.at[k]
            ).start()

        @pl.when(w < WIDE // 2)
        def _():
            pltpu.make_async_copy(
                csend.at[k, pl.ds(2 * w, 1)], crecv.at[k, pl.ds(2 * w, 1)], c_recv.at[k]
            ).start()

        def give(t, carry):
            to = lax.rem(w + t, WIDE)

            def go(count):
                pltpu.make_async_remote_copy(
                    src_ref=csend.at[k, pl.ds(2 * to, count)],
                    dst_ref=crecv.at[k, pl.ds(2 * w, count)],
                    send_sem=c_send.at[k], recv_sem=c_recv.at[k],
                    device_id=(to, n), device_id_type=MESH,
                ).start()

            @pl.when(to >= WIDE // 2)
            def _():
                go(2)

            @pl.when(to < WIDE // 2)
            def _():
                go(1)

            return carry

        lax.fori_loop(1, WIDE, give, 0)

    for k in range(NCH):
        transform(k)
        if k:
            spectral(k - 1)
    spectral(NCH - 1)

    def drain(ref, sem):
        pltpu.make_async_copy(ref, ref, sem).wait()

    for k in range(NCH):
        drain(arecv.at[k, pl.ds(0, 15)], a_send.at[k])
        drain(brecv.at[k], b_send.at[k])

        @pl.when(w >= WIDE // 2)
        def _():
            drain(csend.at[k, pl.ds(0, 46)], c_send.at[k])
            drain(crecv.at[k], c_recv.at[k])

        @pl.when(w < WIDE // 2)
        def _():
            drain(csend.at[k, pl.ds(0, 47)], c_send.at[k])
            drain(crecv.at[k, pl.ds(0, 32)], c_recv.at[k])
    inv_out.wait()


def solve_kernel(where, x_ref, inv_ref, out_ref):
    keep = where[0] >= WIDE // 2
    vals = x_ref[...].astype(F32)
    lane = vals.reshape(2, CHIPS, 2, 2, 2, 8, 128)
    for e in range(2):
        blocks = []
        for half in range(2):
            for g in range(2):
                lo = lane[g, :, half, 0, e]
                hi = jnp.where(keep, lane[g, :, half, 1, e], 0.0)
                both = jnp.stack([lo, hi], axis=1)
                blocks.append(both.reshape(CHIPS * 16, 128).astype(BF16))
        lhs = jnp.concatenate(blocks, axis=1)
        got = jnp.dot(lhs, inv_ref[e], preferred_element_type=F32)
        got = got.reshape(CHIPS, 2, 8, 512)
        lo, hi = got[:, 0], got[:, 1]
        first = jnp.concatenate([lo[:, :4], hi[:, :4]], axis=1)
        second = jnp.concatenate([lo[:, 4:], hi[:, 4:]], axis=1)
        out_ref[e, 0] = jnp.stack([first, second], axis=1).reshape(256, 512)


def per_device(field, table, inverse, modes):
    fields = field.reshape(16, 2, CHIPS, 16, TB)
    modes_rows = jnp.broadcast_to(modes[:, None], (8, 128))
    any_spec = pl.BlockSpec(memory_space=pl.ANY)
    vmem_spec = pl.BlockSpec(memory_space=pltpu.VMEM)
    dma = pltpu.SemaphoreType.DMA
    crecv, invt = pl.pallas_call(
        transform_kernel,
        name="transform",
        out_shape=(
            jax.ShapeDtypeStruct((NCH, 2 * WIDE, 64, 128), BF16),
            jax.ShapeDtypeStruct((8, 512, 512), BF16),
        ),
        in_specs=[any_spec, any_spec, vmem_spec, any_spec],
        out_specs=(any_spec, any_spec),
        scratch_shapes=[
            pltpu.VMEM((NCH, CHIPS, 8, 16, TB), BF16),
            pltpu.VMEM((2, 8, DEG, TB), BF16),
            pltpu.VMEM((2, 8, 128), jnp.int32),
            pltpu.VMEM((16, 128, TB), BF16),
            pltpu.VMEM((2, 2, DEG, 128), F32),
            pltpu.VMEM((NCH, NARROW, ROWS, 128), BF16),
            pltpu.VMEM((NCH, NARROW - 1, ROWS, 128), BF16),
            pltpu.VMEM((NCH, 2 * WIDE, 64, 128), BF16),
            pltpu.VMEM((8, 512, 512), BF16),
            pltpu.VMEM((8, 512, 512), BF16),
            pltpu.VMEM((512, 512), BF16),
            dma((NCH,)), dma((NCH,)), dma((6,)), dma((NCH,)), dma((NCH,)),
            dma((NCH,)), dma((NCH,)), dma((2,)),
        ],
        compiler_params=pltpu.CompilerParams(
            collective_id=0, has_side_effects=True, vmem_limit_bytes=60 * 2**20
        ),
    )(fields, table, modes_rows, inverse)
    x = crecv.reshape(NCH, CHIPS, 2, 2, 64, 128)
    where = lax.axis_index("wide").astype(jnp.int32).reshape(1)
    return pl.pallas_call(
        solve_kernel,
        name="solve",
        out_shape=jax.ShapeDtypeStruct((8, 2, 256, 512), F32),
        grid_spec=pltpu.PrefetchScalarGridSpec(
            num_scalar_prefetch=1,
            grid=(4, 2),
            in_specs=[
                pl.BlockSpec((2, CHIPS, 2, 2, 16, 128), lambda i, c, s: (c, 0, 0, 0, i, 0)),
                pl.BlockSpec((2, 512, 512), lambda i, c, s: (i, 0, 0)),
            ],
            out_specs=pl.BlockSpec((2, 1, 256, 512), lambda i, c, s: (i, c, 0, 0)),
        ),
        compiler_params=pltpu.CompilerParams(vmem_limit_bytes=48 * 2**20),
    )(where, x, invt)


def solution(mesh):
    placed = (
        P("wide", None, None, "narrow"),
        P("wide", None, "narrow"),
        P(("wide", "narrow"), None, None),
        P("wide"),
    )
    return jax.shard_map(
        per_device,
        mesh=mesh,
        in_specs=placed,
        out_specs=P(("wide", "narrow"), None, None, None),
        check_vma=False,
    )
```

```python
import functools

import jax
import jax.numpy as jnp
from jax import lax
from jax.experimental import pallas as pl
from jax.experimental.pallas import tpu as pltpu
from jax.sharding import PartitionSpec as P

MESH = pl.DeviceIdType.MESH
BF16 = jnp.bfloat16
F32 = jnp.float32

WIDE = 32
NARROW = 4
CHIPS = 16
DEG = 1024
POS = 33
ROWS = POS * 64
HALF = ROWS // 2
NCH = 4
TB = 384

PLANE = [
    (0, 1), (1, 0), (0, 3), (3, 0), (1, 1), (3, 3), (1, 3), (3, 1),
    (0, 2), (2, 0), (1, 2), (2, 1), (3, 2), (2, 3), (2, 2),
]


def transform_kernel(
    field, table, modes, inverse,
    crecv, invt,
    arecv, tabv, modv, ft, res, pbuf, brecv, bpass, csend, invv, invo, perm,
    a_send, a_recv, t_sem, b_send, b_recv, c_send, c_recv, i_sem,
):
    w = lax.axis_index("wide")
    n = lax.axis_index("narrow")
    q = w // 2
    core = w % 2
    y = q // 4
    z = q % 4
    sib = w + 1 - 2 * core

    own_table = pltpu.make_async_copy(table, tabv.at[core], t_sem.at[0])
    own_table.start()
    own_modes = pltpu.make_async_copy(modes, modv.at[core], t_sem.at[1])
    own_modes.start()
    inv_in = pltpu.make_async_copy(inverse, invv, i_sem.at[0])
    inv_in.start()
    for k in range(NCH):
        pltpu.make_async_copy(
            field.at[pl.ds(8 * (k % 2), 8), k // 2, q], arecv.at[k, q], a_recv.at[k]
        ).start()

    barrier = pltpu.get_barrier_semaphore()

    def greet(t, carry):
        pl.semaphore_signal(
            barrier, inc=1, device_id=(lax.rem(w + t, WIDE), n), device_id_type=MESH
        )
        return carry

    lax.fori_loop(1, WIDE, greet, 0)
    for d in range(1, NARROW):
        pl.semaphore_signal(
            barrier, inc=1, device_id=(w, lax.rem(n + d, NARROW)), device_id_type=MESH
        )
    pl.semaphore_wait(barrier, WIDE - 1 + NARROW - 1)

    def send_field(k):
        for dy, dz in PLANE:
            peer = lax.rem(y + dy, 4) * 4 + lax.rem(z + dz, 4)
            pltpu.make_async_remote_copy(
                src_ref=field.at[pl.ds(8 * (k % 2), 8), k // 2, peer],
                dst_ref=arecv.at[k, q],
                send_sem=a_send.at[k],
                recv_sem=a_recv.at[k],
                device_id=(peer * 2 + core, n),
                device_id_type=MESH,
            ).start()

    give_modes = pltpu.make_async_remote_copy(
        src_ref=modes, dst_ref=modv.at[core], send_sem=t_sem.at[2],
        recv_sem=t_sem.at[3], device_id=(sib, n), device_id_type=MESH,
    )
    give_modes.start()
    give_table = pltpu.make_async_remote_copy(
        src_ref=table, dst_ref=tabv.at[core], send_sem=t_sem.at[4],
        recv_sem=t_sem.at[5], device_id=(sib, n), device_id_type=MESH,
    )
    send_field(0)
    give_table.start()
    send_field(1)

    inv_in.wait()
    arrive = lax.broadcasted_iota(jnp.int32, (512, 512), 0)
    natural = (
        ((arrive // 8) % 16) * 32 + (arrive // 256) * 16 + ((arrive // 128) % 2) * 8 + arrive % 8
    )
    radius = lax.broadcasted_iota(jnp.int32, (512, 512), 1)
    perm[...] = jnp.where(radius == natural, 1.0, 0.0).astype(BF16)

    def reorder(t, carry):
        invo[t] = lax.dot_general(
            perm[...], invv[t], (((1,), (1,)), ((), ())), preferred_element_type=F32
        ).astype(BF16)
        return carry

    lax.fori_loop(0, 8, reorder, 0)
    inv_out = pltpu.make_async_copy(invo, invt, i_sem.at[1])
    inv_out.start()

    own_table.wait()
    own_modes.wait()
    give_modes.wait()
    give_table.wait()

    right, opposite, left = (lax.rem(n + d, NARROW) for d in range(1, NARROW))

    def landed(ref, sem):
        pltpu.make_async_copy(ref, ref, sem).wait()

    def hop(src, dst, to, send_sem, recv_sem):
        pltpu.make_async_remote_copy(
            src_ref=src, dst_ref=dst, send_sem=send_sem, recv_sem=recv_sem,
            device_id=(w, to), device_id_type=MESH,
        ).start()

    def transform(k):
        landed(arecv.at[k], a_recv.at[k])
        if k + 2 < NCH:
            send_field(k + 2)

        def turn(t, carry):
            block = arecv[k, pl.ds(2 * t, 2)].reshape(16, 16, TB)
            ft[:, pl.ds(pl.multiple_of(16 * t, 16), 16), :] = jnp.swapaxes(block, 0, 1)
            return carry

        lax.fori_loop(0, 8, turn, 0)

        def two_pairs(pp, carry):
            side = pp // 2
            first = 2 * (pp % 2)
            for e in range(2):
                for kind in range(2):
                    slot = first + e + 4 * kind
                    res[e, kind] = lax.dot_general(
                        tabv[side, slot], ft[side * 8 + slot],
                        (((1,), (1,)), ((), ())), preferred_element_type=F32,
                    )

            at32 = lax.broadcasted_iota(jnp.int32, (32, 128), 0)

            def part(e, kind, block):
                rows = res[e, kind, pl.ds(pl.multiple_of(block * 32, 32), 32), :]
                m = modv[side, pl.ds(first + e + 4 * kind, 1), :]
                return jnp.where(at32 + block * 32 >= m, rows, 0.0)

            def put(pos, vals):
                for t in range(NARROW):
                    both = jnp.concatenate([v[8 * t:8 * t + 8] for v in vals], axis=0)
                    pbuf[k, t, pl.ds(pl.multiple_of(pos * 64 + pp * 16, 16), 16), :] = (
                        both.astype(BF16)
                    )

            put(0, [part(e, 1, 31) for e in range(2)])
            put(32, [part(e, 0, 31) for e in range(2)])

            def fold(v, c2):
                put(v + 1, [part(e, 0, v) + part(e, 1, 30 - v) for e in range(2)])
                return c2

            lax.fori_loop(0, 31, fold, 0)
            return carry

        lax.fori_loop(0, 4, two_pairs, 0)
        hop(pbuf.at[k, opposite, pl.ds(0, HALF)], bpass.at[k, 0], right, b_send.at[k, 0], b_recv.at[k, 0])
        hop(pbuf.at[k, opposite, pl.ds(HALF, HALF)], bpass.at[k, 1], left, b_send.at[k, 1], b_recv.at[k, 1])
        hop(pbuf.at[k, right, pl.ds(HALF, HALF)], brecv.at[k, 0, pl.ds(HALF, HALF)], right, b_send.at[k, 2], b_recv.at[k, 2])
        hop(pbuf.at[k, left, pl.ds(0, HALF)], brecv.at[k, 1, pl.ds(0, HALF)], left, b_send.at[k, 3], b_recv.at[k, 3])

    def combine(k):
        for way, (to, base) in enumerate(((right, 0), (left, HALF))):
            landed(bpass.at[k, way], b_recv.at[k, way])

            def add(t, carry):
                here = pl.ds(pl.multiple_of(base + t * 96, 32), 96)
                there = pl.ds(pl.multiple_of(t * 96, 32), 96)
                pbuf[k, to, here, :] = (
                    pbuf[k, to, here, :].astype(F32) + bpass[k, way, there, :].astype(F32)
                ).astype(BF16)
                return carry

            lax.fori_loop(0, HALF // 96, add, 0)
            half = pl.ds(base, HALF)
            hop(pbuf.at[k, to, half], brecv.at[k, way, half], to, b_send.at[k, 4 + way], b_recv.at[k, 4 + way])

    def spectral(k):
        landed(brecv.at[k, 0, pl.ds(HALF, HALF)], b_recv.at[k, 2])
        landed(brecv.at[k, 1, pl.ds(0, HALF)], b_recv.at[k, 3])
        landed(brecv.at[k, 0, pl.ds(0, HALF)], b_recv.at[k, 4])
        landed(brecv.at[k, 1, pl.ds(HALF, HALF)], b_recv.at[k, 5])

        def modes_of(kind):
            return jnp.concatenate(
                [modv[s, 4 * kind:4 * kind + 4, :] for s in range(2)], axis=0
            )

        lo_modes, hi_modes = modes_of(0), modes_of(1)
        at = lax.broadcasted_iota(jnp.int32, (8, 8, 128), 0)

        def put(pos, v, kind, m):
            rows = pl.ds(pl.multiple_of(pos * 64, 64), 64)
            total = pbuf[k, n, rows, :].astype(F32)
            for d in range(2):
                total = total + brecv[k, d, rows, :].astype(F32)
            turned = jnp.swapaxes(total.reshape(8, 8, 128), 0, 1)
            kept = jnp.where(at + (v * 32 + n * 8) >= m[None], turned, 0.0)
            csend[k, 2 * v + kind] = kept.reshape(64, 128).astype(BF16)

        def low(v, carry):
            put(v + 1, v, 0, lo_modes)
            return carry

        def high(v, carry):
            put(31 - v, v, 1, hi_modes)
            return carry

        lax.fori_loop(0, WIDE, low, 0)
        lax.fori_loop(WIDE // 2, WIDE, high, 0)

        @pl.when(w >= WIDE // 2)
        def _():
            pltpu.make_async_copy(
                csend.at[k, pl.ds(2 * w, 2)], crecv.at[k, pl.ds(2 * w, 2)], c_recv.at[k]
            ).start()

        @pl.when(w < WIDE // 2)
        def _():
            pltpu.make_async_copy(
                csend.at[k, pl.ds(2 * w, 1)], crecv.at[k, pl.ds(2 * w, 1)], c_recv.at[k]
            ).start()

        def give(t, carry):
            to = lax.rem(w + t, WIDE)

            def go(count):
                pltpu.make_async_remote_copy(
                    src_ref=csend.at[k, pl.ds(2 * to, count)],
                    dst_ref=crecv.at[k, pl.ds(2 * w, count)],
                    send_sem=c_send.at[k], recv_sem=c_recv.at[k],
                    device_id=(to, n), device_id_type=MESH,
                ).start()

            @pl.when(to >= WIDE // 2)
            def _():
                go(2)

            @pl.when(to < WIDE // 2)
            def _():
                go(1)

            return carry

        lax.fori_loop(1, WIDE, give, 0)

    for k in range(NCH):
        transform(k)
        if k:
            spectral(k - 1)
        combine(k)
    spectral(NCH - 1)

    for k in range(NCH):
        landed(arecv.at[k, pl.ds(0, 15)], a_send.at[k])
        for i in range(6):
            landed(bpass.at[k, 0], b_send.at[k, i])

        @pl.when(w >= WIDE // 2)
        def _():
            landed(csend.at[k, pl.ds(0, 46)], c_send.at[k])
            landed(crecv.at[k], c_recv.at[k])

        @pl.when(w < WIDE // 2)
        def _():
            landed(csend.at[k, pl.ds(0, 47)], c_send.at[k])
            landed(crecv.at[k, pl.ds(0, 32)], c_recv.at[k])
    inv_out.wait()


def solve_kernel(where, x_ref, inv_ref, out_ref):
    keep = where[0] >= WIDE // 2
    vals = x_ref[...].astype(F32)
    lane = vals.reshape(2, CHIPS, 2, 2, 2, 8, 128)
    for e in range(2):
        blocks = []
        for half in range(2):
            for g in range(2):
                lo = lane[g, :, half, 0, e]
                hi = jnp.where(keep, lane[g, :, half, 1, e], 0.0)
                both = jnp.stack([lo, hi], axis=1)
                blocks.append(both.reshape(CHIPS * 16, 128).astype(BF16))
        lhs = jnp.concatenate(blocks, axis=1)
        got = jnp.dot(lhs, inv_ref[e], preferred_element_type=F32)
        got = got.reshape(CHIPS, 2, 8, 512)
        lo, hi = got[:, 0], got[:, 1]
        first = jnp.concatenate([lo[:, :4], hi[:, :4]], axis=1)
        second = jnp.concatenate([lo[:, 4:], hi[:, 4:]], axis=1)
        out_ref[e, 0] = jnp.stack([first, second], axis=1).reshape(256, 512)


def per_device(field, table, inverse, modes):
    fields = field.reshape(16, 2, CHIPS, 16, TB)
    modes_rows = jnp.broadcast_to(modes[:, None], (8, 128))
    any_spec = pl.BlockSpec(memory_space=pl.ANY)
    vmem_spec = pl.BlockSpec(memory_space=pltpu.VMEM)
    dma = pltpu.SemaphoreType.DMA
    crecv, invt = pl.pallas_call(
        transform_kernel,
        name="transform",
        out_shape=(
            jax.ShapeDtypeStruct((NCH, 2 * WIDE, 64, 128), BF16),
            jax.ShapeDtypeStruct((8, 512, 512), BF16),
        ),
        in_specs=[any_spec, any_spec, vmem_spec, any_spec],
        out_specs=(any_spec, any_spec),
        scratch_shapes=[
            pltpu.VMEM((NCH, CHIPS, 8, 16, TB), BF16),
            pltpu.VMEM((2, 8, DEG, TB), BF16),
            pltpu.VMEM((2, 8, 128), jnp.int32),
            pltpu.VMEM((16, 128, TB), BF16),
            pltpu.VMEM((2, 2, DEG, 128), F32),
            pltpu.VMEM((NCH, NARROW, ROWS, 128), BF16),
            pltpu.VMEM((NCH, 2, ROWS, 128), BF16),
            pltpu.VMEM((NCH, 2, HALF, 128), BF16),
            pltpu.VMEM((NCH, 2 * WIDE, 64, 128), BF16),
            pltpu.VMEM((8, 512, 512), BF16),
            pltpu.VMEM((8, 512, 512), BF16),
            pltpu.VMEM((512, 512), BF16),
            dma((NCH,)), dma((NCH,)), dma((6,)), dma((NCH, 6)), dma((NCH, 6)),
            dma((NCH,)), dma((NCH,)), dma((2,)),
        ],
        compiler_params=pltpu.CompilerParams(
            collective_id=0, has_side_effects=True, vmem_limit_bytes=60 * 2**20
        ),
    )(fields, table, modes_rows, inverse)
    x = crecv.reshape(NCH, CHIPS, 2, 2, 64, 128)
    where = lax.axis_index("wide").astype(jnp.int32).reshape(1)
    return pl.pallas_call(
        solve_kernel,
        name="solve",
        out_shape=jax.ShapeDtypeStruct((8, 2, 256, 512), F32),
        grid_spec=pltpu.PrefetchScalarGridSpec(
            num_scalar_prefetch=1,
            grid=(4, 2),
            in_specs=[
                pl.BlockSpec((2, CHIPS, 2, 2, 16, 128), lambda i, c, s: (c, 0, 0, 0, i, 0)),
                pl.BlockSpec((2, 512, 512), lambda i, c, s: (i, 0, 0)),
            ],
            out_specs=pl.BlockSpec((2, 1, 256, 512), lambda i, c, s: (i, c, 0, 0)),
        ),
        compiler_params=pltpu.CompilerParams(vmem_limit_bytes=48 * 2**20),
    )(where, x, invt)


def solution(mesh):
    placed = (
        P("wide", None, None, "narrow"),
        P("wide", None, "narrow"),
        P(("wide", "narrow"), None, None),
        P("wide"),
    )
    return jax.shard_map(
        per_device,
        mesh=mesh,
        in_specs=placed,
        out_specs=P(("wide", "narrow"), None, None, None),
        check_vma=False,
    )
```

```python
import functools

import jax
import jax.numpy as jnp
from jax import lax
from jax.experimental import pallas as pl
from jax.experimental.pallas import tpu as pltpu
from jax.sharding import PartitionSpec as P

MESH = pl.DeviceIdType.MESH
BF16 = jnp.bfloat16
F32 = jnp.float32

WIDE = 32
NARROW = 4
CHIPS = 16
DEG = 1024
POS = 33
ROWS = POS * 64
HALF = ROWS // 2
NCH = 4
TB = 384

PLANE = [
    (0, 1), (1, 0), (0, 3), (3, 0), (1, 1), (3, 3), (1, 3), (3, 1),
    (0, 2), (2, 0), (1, 2), (2, 1), (3, 2), (2, 3), (2, 2),
]


def transform_kernel(
    field, table, modes, inverse,
    crecv, invt,
    arecv, tabv, modv, ft, res, pbuf, brecv, bpass, csend, invv, invo, perm,
    a_send, a_recv, t_sem, b_send, b_recv, c_send, c_recv, i_sem,
):
    w = lax.axis_index("wide")
    n = lax.axis_index("narrow")
    q = w // 2
    core = w % 2
    y = q // 4
    z = q % 4
    sib = w + 1 - 2 * core

    own_table = pltpu.make_async_copy(table, tabv.at[core], t_sem.at[0])
    own_table.start()
    for i in range(8):
        modv[core, i, :] = jnp.full((128,), modes[i], jnp.int32)
    inv_in = pltpu.make_async_copy(inverse, invv, i_sem.at[0])
    inv_in.start()
    for k in range(NCH):
        pltpu.make_async_copy(
            field.at[pl.ds(8 * (k % 2), 8), k // 2, q], arecv.at[k, q], a_recv.at[k]
        ).start()

    barrier = pltpu.get_barrier_semaphore()

    def greet(t, carry):
        pl.semaphore_signal(
            barrier, inc=1, device_id=(lax.rem(w + t, WIDE), n), device_id_type=MESH
        )
        return carry

    lax.fori_loop(1, WIDE, greet, 0)
    for d in range(1, NARROW):
        pl.semaphore_signal(
            barrier, inc=1, device_id=(w, lax.rem(n + d, NARROW)), device_id_type=MESH
        )
    pl.semaphore_wait(barrier, WIDE - 1 + NARROW - 1)

    def send_field(k):
        for dy, dz in PLANE:
            peer = lax.rem(y + dy + core * (4 - 2 * dy), 4) * 4 + lax.rem(z + dz + core * (4 - 2 * dz), 4)
            pltpu.make_async_remote_copy(
                src_ref=field.at[pl.ds(8 * (k % 2), 8), k // 2, peer],
                dst_ref=arecv.at[k, q],
                send_sem=a_send.at[k],
                recv_sem=a_recv.at[k],
                device_id=(peer * 2 + core, n),
                device_id_type=MESH,
            ).start()

    give_modes = pltpu.make_async_remote_copy(
        src_ref=modv.at[core], dst_ref=modv.at[core], send_sem=t_sem.at[2],
        recv_sem=t_sem.at[3], device_id=(sib, n), device_id_type=MESH,
    )
    give_modes.start()
    give_table = pltpu.make_async_remote_copy(
        src_ref=table, dst_ref=tabv.at[core], send_sem=t_sem.at[4],
        recv_sem=t_sem.at[5], device_id=(sib, n), device_id_type=MESH,
    )
    send_field(0)
    give_table.start()
    send_field(1)

    inv_in.wait()
    arrive = lax.broadcasted_iota(jnp.int32, (512, 512), 0)
    natural = (
        ((arrive // 8) % 16) * 32 + (arrive // 256) * 16 + ((arrive // 128) % 2) * 8 + arrive % 8
    )
    radius = lax.broadcasted_iota(jnp.int32, (512, 512), 1)
    perm[...] = jnp.where(radius == natural, 1.0, 0.0).astype(BF16)

    def reorder(t, carry):
        invo[t] = lax.dot_general(
            perm[...], invv[t], (((1,), (1,)), ((), ())), preferred_element_type=F32
        ).astype(BF16)
        return carry

    lax.fori_loop(0, 8, reorder, 0)
    inv_out = pltpu.make_async_copy(invo, invt, i_sem.at[1])
    inv_out.start()

    own_table.wait()
    give_modes.wait()
    give_table.wait()

    right, opposite, left = (lax.rem(n + d, NARROW) for d in range(1, NARROW))

    def landed(ref, sem):
        pltpu.make_async_copy(ref, ref, sem).wait()

    def hop(src, dst, to, send_sem, recv_sem):
        pltpu.make_async_remote_copy(
            src_ref=src, dst_ref=dst, send_sem=send_sem, recv_sem=recv_sem,
            device_id=(w, to), device_id_type=MESH,
        ).start()

    def transform(k):
        landed(arecv.at[k], a_recv.at[k])
        if k + 2 < NCH:
            send_field(k + 2)

        def turn(t, carry):
            block = arecv[k, pl.ds(2 * t, 2)].reshape(16, 16, TB)
            ft[:, pl.ds(pl.multiple_of(16 * t, 16), 16), :] = jnp.swapaxes(block, 0, 1)
            return carry

        lax.fori_loop(0, 8, turn, 0)

        def two_pairs(pp, carry):
            side = pp // 2
            first = 2 * (pp % 2)
            for e in range(2):
                for kind in range(2):
                    slot = first + e + 4 * kind
                    res[e, kind] = lax.dot_general(
                        tabv[side, slot], ft[side * 8 + slot],
                        (((1,), (1,)), ((), ())), preferred_element_type=F32,
                    )

            at32 = lax.broadcasted_iota(jnp.int32, (32, 128), 0)

            def part(e, kind, block):
                rows = res[e, kind, pl.ds(pl.multiple_of(block * 32, 32), 32), :]
                m = modv[side, pl.ds(first + e + 4 * kind, 1), :]
                return jnp.where(at32 + block * 32 >= m, rows, 0.0)

            def put(pos, vals):
                for t in range(NARROW):
                    both = jnp.concatenate([v[8 * t:8 * t + 8] for v in vals], axis=0)
                    pbuf[k, t, pl.ds(pl.multiple_of(pos * 64 + pp * 16, 16), 16), :] = (
                        both.astype(BF16)
                    )

            put(0, [part(e, 1, 31) for e in range(2)])
            put(32, [part(e, 0, 31) for e in range(2)])

            def fold(v, c2):
                put(v + 1, [part(e, 0, v) + part(e, 1, 30 - v) for e in range(2)])
                return c2

            lax.fori_loop(0, 31, fold, 0)
            return carry

        lax.fori_loop(0, 4, two_pairs, 0)
        hop(pbuf.at[k, opposite, pl.ds(0, HALF)], bpass.at[k, 0], right, b_send.at[k, 0], b_recv.at[k, 0])
        hop(pbuf.at[k, opposite, pl.ds(HALF, HALF)], bpass.at[k, 1], left, b_send.at[k, 1], b_recv.at[k, 1])
        hop(pbuf.at[k, right, pl.ds(HALF, HALF)], brecv.at[k, 0, pl.ds(HALF, HALF)], right, b_send.at[k, 2], b_recv.at[k, 2])
        hop(pbuf.at[k, left, pl.ds(0, HALF)], brecv.at[k, 1, pl.ds(0, HALF)], left, b_send.at[k, 3], b_recv.at[k, 3])

    def combine(k):
        for way, (to, base) in enumerate(((right, 0), (left, HALF))):
            landed(bpass.at[k, way], b_recv.at[k, way])

            def add(t, carry):
                here = pl.ds(pl.multiple_of(base + t * 96, 32), 96)
                there = pl.ds(pl.multiple_of(t * 96, 32), 96)
                pbuf[k, to, here, :] = (
                    pbuf[k, to, here, :].astype(F32) + bpass[k, way, there, :].astype(F32)
                ).astype(BF16)
                return carry

            lax.fori_loop(0, HALF // 96, add, 0)
            half = pl.ds(base, HALF)
            hop(pbuf.at[k, to, half], brecv.at[k, way, half], to, b_send.at[k, 4 + way], b_recv.at[k, 4 + way])

    def spectral(k):
        landed(brecv.at[k, 0, pl.ds(HALF, HALF)], b_recv.at[k, 2])
        landed(brecv.at[k, 1, pl.ds(0, HALF)], b_recv.at[k, 3])
        landed(brecv.at[k, 0, pl.ds(0, HALF)], b_recv.at[k, 4])
        landed(brecv.at[k, 1, pl.ds(HALF, HALF)], b_recv.at[k, 5])

        def modes_of(kind):
            return jnp.concatenate(
                [modv[s, 4 * kind:4 * kind + 4, :] for s in range(2)], axis=0
            )

        lo_modes, hi_modes = modes_of(0), modes_of(1)
        at = lax.broadcasted_iota(jnp.int32, (8, 8, 128), 0)

        upper = lax.broadcasted_iota(jnp.int32, (8, 8, 128), 1) < 4

        def total(pos, v, m):
            rows = pl.ds(pl.multiple_of(pos * 64, 64), 64)
            vals = pbuf[k, n, rows, :].astype(F32)
            for d in range(2):
                vals = vals + brecv[k, d, rows, :].astype(F32)
            turned = jnp.swapaxes(vals.reshape(8, 8, 128), 0, 1)
            return jnp.where(at + (v * 32 + n * 8) >= m[None], turned, 0.0)

        def low(v, carry):
            csend[k, v, pl.ds(0, 64), :] = total(v + 1, v, lo_modes).reshape(64, 128).astype(BF16)
            return carry

        def high(v, carry):
            lo = total(v + 1, v, lo_modes)
            hi = total(31 - v, v, hi_modes)
            first = jnp.where(upper, lo, pltpu.roll(hi, 4, 1))
            second = jnp.where(upper, pltpu.roll(lo, 4, 1), hi)
            both = jnp.concatenate([first, second], axis=1).reshape(128, 128)
            csend[k, v] = both.astype(BF16)
            return carry

        lax.fori_loop(0, WIDE // 2, low, 0)
        lax.fori_loop(WIDE // 2, WIDE, high, 0)

        target = crecv.at[k, q, core]

        def keep(count):
            pltpu.make_async_copy(
                csend.at[k, w, pl.ds(0, count)], target.at[pl.ds(0, count)], c_recv.at[k]
            ).start()

        @pl.when(w >= WIDE // 2)
        def _():
            keep(128)

        @pl.when(w < WIDE // 2)
        def _():
            keep(64)

        def give(t, carry):
            to = lax.rem(w + 11 * t, WIDE)

            def go(count):
                pltpu.make_async_remote_copy(
                    src_ref=csend.at[k, to, pl.ds(0, count)],
                    dst_ref=target.at[pl.ds(0, count)],
                    send_sem=c_send.at[k], recv_sem=c_recv.at[k],
                    device_id=(to, n), device_id_type=MESH,
                ).start()

            @pl.when(to >= WIDE // 2)
            def _():
                go(128)

            @pl.when(to < WIDE // 2)
            def _():
                go(64)

            return carry

        lax.fori_loop(1, WIDE, give, 0)

    def received(k):
        @pl.when(w >= WIDE // 2)
        def _():
            landed(crecv.at[k], c_recv.at[k])

        @pl.when(w < WIDE // 2)
        def _():
            landed(crecv.at[k, :, :, pl.ds(0, 64)], c_recv.at[k])

    for k in range(NCH):
        transform(k)
        if k:
            spectral(k - 1)
        combine(k)
    spectral(NCH - 1)
    for k in range(NCH):
        received(k)

    for k in range(NCH):
        landed(arecv.at[k, pl.ds(0, 15)], a_send.at[k])
        for i in range(6):
            landed(bpass.at[k, 0], b_send.at[k, i])

        @pl.when(w >= WIDE // 2)
        def _():
            landed(csend.at[k, pl.ds(0, 23)], c_send.at[k])

        @pl.when(w < WIDE // 2)
        def _():
            landed(csend.at[k, pl.ds(0, 23)], c_send.at[k])
            landed(csend.at[k, 0, pl.ds(0, 64)], c_send.at[k])
    inv_out.wait()


def solve_upper(x, inv, c, t):
    rows = pl.ds(pl.multiple_of(t * 16, 16), 16)
    blocks = [
        x[2 * c + g, :, half, rows, :].reshape(CHIPS * 16, 128)
        for half in range(2) for g in range(2)
    ]
    return jnp.dot(jnp.concatenate(blocks, axis=1), inv[t], preferred_element_type=F32)


def solve_lower(x, inv, c, t):
    rows = pl.ds(pl.multiple_of((t // 2) * 16, 16), 16)
    even = lax.broadcasted_iota(jnp.int32, (CHIPS, 8, 128), 1) * 0 + t % 2 == 0
    blocks = []
    for half in range(2):
        for g in range(2):
            two = x[2 * c + g, :, half, rows, :].astype(F32)
            one = jnp.where(even, two[:, :8], two[:, 8:])
            blocks.append(one.reshape(CHIPS * 8, 128).astype(BF16))
    got = jnp.dot(
        jnp.concatenate(blocks, axis=1), inv[t], preferred_element_type=F32
    ).reshape(CHIPS, 8, 512)
    upper = lax.broadcasted_iota(jnp.int32, (CHIPS, 8, 512), 1) < 4
    first = jnp.where(upper, got, 0.0)
    second = jnp.where(upper, pltpu.roll(got, 4, 1), 0.0)
    return jnp.concatenate([first, second], axis=1).reshape(256, 512)


def solve_kernel(where, x, inv, solved, xv, invv, outv, x_sem, i_sem, o_sem):
    def run(rows, solve):
        copies = [
            pltpu.make_async_copy(
                x.at[k, :, half, pl.ds(0, rows)], xv.at[k, :, half, pl.ds(0, rows)],
                x_sem.at[k, half],
            )
            for k in range(NCH) for half in range(2)
        ]
        for copy in copies[:4]:
            copy.start()

        def fetch(t, carry):
            pltpu.make_async_copy(inv.at[t], invv.at[t], i_sem.at[t]).start()
            return carry

        lax.fori_loop(0, 8, fetch, 0)
        for copy in copies[4:]:
            copy.start()
        for c in range(2):
            for copy in copies[4 * c:4 * c + 4]:
                copy.wait()

            def degree(t, carry):
                if c == 0:
                    pltpu.make_async_copy(inv.at[t], invv.at[t], i_sem.at[t]).wait()
                outv[c, t] = solve(xv, invv, c, t)
                pltpu.make_async_copy(outv.at[c, t], solved.at[t, c], o_sem).start()
                return carry

            lax.fori_loop(0, 8, degree, 0)

    @pl.when(where[0] >= WIDE // 2)
    def _():
        run(128, solve_upper)

    @pl.when(where[0] < WIDE // 2)
    def _():
        run(64, solve_lower)

    pltpu.make_async_copy(outv, outv, o_sem).wait()


def per_device(field, table, inverse, modes):
    fields = field.reshape(16, 2, CHIPS, 16, TB)
    any_spec = pl.BlockSpec(memory_space=pl.ANY)
    dma = pltpu.SemaphoreType.DMA
    crecv, invt = pl.pallas_call(
        transform_kernel,
        name="transform",
        out_shape=(
            jax.ShapeDtypeStruct((NCH, CHIPS, 2, 128, 128), BF16),
            jax.ShapeDtypeStruct((8, 512, 512), BF16),
        ),
        in_specs=[any_spec, any_spec, pl.BlockSpec(memory_space=pltpu.SMEM), any_spec],
        out_specs=(any_spec, any_spec),
        scratch_shapes=[
            pltpu.VMEM((NCH, CHIPS, 8, 16, TB), BF16),
            pltpu.VMEM((2, 8, DEG, TB), BF16),
            pltpu.VMEM((2, 8, 128), jnp.int32),
            pltpu.VMEM((16, 128, TB), BF16),
            pltpu.VMEM((2, 2, DEG, 128), F32),
            pltpu.VMEM((NCH, NARROW, ROWS, 128), BF16),
            pltpu.VMEM((NCH, 2, ROWS, 128), BF16),
            pltpu.VMEM((NCH, 2, HALF, 128), BF16),
            pltpu.VMEM((NCH, WIDE, 128, 128), BF16),
            pltpu.VMEM((8, 512, 512), BF16),
            pltpu.VMEM((8, 512, 512), BF16),
            pltpu.VMEM((512, 512), BF16),
            dma((NCH,)), dma((NCH,)), dma((6,)), dma((NCH, 6)), dma((NCH, 6)),
            dma((NCH,)), dma((NCH,)), dma((2,)),
        ],
        compiler_params=pltpu.CompilerParams(
            collective_id=0, has_side_effects=True, vmem_limit_bytes=60 * 2**20
        ),
    )(fields, table, modes, inverse)
    where = lax.axis_index("wide").astype(jnp.int32).reshape(1)
    return pl.pallas_call(
        solve_kernel,
        name="solve",
        out_shape=jax.ShapeDtypeStruct((8, 2, 256, 512), F32),
        in_specs=[pl.BlockSpec(memory_space=pltpu.SMEM), any_spec, any_spec],
        out_specs=any_spec,
        scratch_shapes=[
            pltpu.VMEM((NCH, CHIPS, 2, 128, 128), BF16),
            pltpu.VMEM((8, 512, 512), BF16),
            pltpu.VMEM((2, 8, 256, 512), F32),
            dma((NCH, 2)), dma((8,)), dma(()),
        ],
        compiler_params=pltpu.CompilerParams(vmem_limit_bytes=60 * 2**20),
    )(where, crecv, invt)


def solution(mesh):
    placed = (
        P("wide", None, None, "narrow"),
        P("wide", None, "narrow"),
        P(("wide", "narrow"), None, None),
        P("wide"),
    )
    return jax.shard_map(
        per_device,
        mesh=mesh,
        in_specs=placed,
        out_specs=P(("wide", "narrow"), None, None, None),
        check_vma=False,
    )
```

```python
import functools

import jax
import jax.numpy as jnp
from jax import lax
from jax.experimental import pallas as pl
from jax.experimental.pallas import tpu as pltpu
from jax.sharding import PartitionSpec as P

MESH = pl.DeviceIdType.MESH
BF16 = jnp.bfloat16
F32 = jnp.float32

WIDE = 32
NARROW = 4
CHIPS = 16
DEG = 1024
POS = 33
ROWS = POS * 64
HALF = ROWS // 2
NCH = 4
TB = 384

PLANE = [(1, 1), (2, 2), (3, 3), (0, 1), (1, 2), (2, 3), (3, 0), (0, 2), (1, 3), (2, 0), (3, 1), (0, 3), (1, 0), (2, 1), (3, 2)]


def transform_kernel(
    field, table, modes, inverse,
    crecv, invt,
    arecv, tabv, modv, ft, res, pbuf, brecv, bpass, csend, invv, invo, perm,
    a_send, a_recv, t_sem, b_send, b_recv, c_send, c_recv, i_sem,
):
    w = lax.axis_index("wide")
    n = lax.axis_index("narrow")
    q = w // 2
    core = w % 2
    y = q // 4
    z = q % 4
    sib = w + 1 - 2 * core

    own_table = pltpu.make_async_copy(table, tabv.at[core], t_sem.at[0])
    own_table.start()
    for i in range(8):
        modv[core, i, :] = jnp.full((128,), modes[i], jnp.int32)
    inv_in = pltpu.make_async_copy(inverse, invv, i_sem.at[0])
    inv_in.start()
    for k in range(NCH):
        pltpu.make_async_copy(
            field.at[pl.ds(8 * (k % 2), 8), k // 2, q], arecv.at[k, q], a_recv.at[k]
        ).start()

    barrier = pltpu.get_barrier_semaphore()

    def greet(t, carry):
        pl.semaphore_signal(
            barrier, inc=1, device_id=(lax.rem(w + t, WIDE), n), device_id_type=MESH
        )
        return carry

    lax.fori_loop(1, WIDE, greet, 0)
    for d in range(1, NARROW):
        pl.semaphore_signal(
            barrier, inc=1, device_id=(w, lax.rem(n + d, NARROW)), device_id_type=MESH
        )
    pl.semaphore_wait(barrier, WIDE - 1 + NARROW - 1)

    def send_field(k):
        for dy, dz in PLANE:
            peer = lax.rem(y + dy + core * (4 - 2 * dy), 4) * 4 + lax.rem(z + dz + core * (4 - 2 * dz), 4)
            pltpu.make_async_remote_copy(
                src_ref=field.at[pl.ds(8 * (k % 2), 8), k // 2, peer],
                dst_ref=arecv.at[k, q],
                send_sem=a_send.at[k],
                recv_sem=a_recv.at[k],
                device_id=(peer * 2 + core, n),
                device_id_type=MESH,
            ).start()

    give_modes = pltpu.make_async_remote_copy(
        src_ref=modv.at[core], dst_ref=modv.at[core], send_sem=t_sem.at[2],
        recv_sem=t_sem.at[3], device_id=(sib, n), device_id_type=MESH,
    )
    give_modes.start()
    give_table = pltpu.make_async_remote_copy(
        src_ref=table, dst_ref=tabv.at[core], send_sem=t_sem.at[4],
        recv_sem=t_sem.at[5], device_id=(sib, n), device_id_type=MESH,
    )
    send_field(0)
    give_table.start()
    send_field(1)

    inv_in.wait()
    arrive = lax.broadcasted_iota(jnp.int32, (512, 512), 0)
    natural = (
        ((arrive // 8) % 16) * 32 + (arrive // 256) * 16 + ((arrive // 128) % 2) * 8 + arrive % 8
    )
    radius = lax.broadcasted_iota(jnp.int32, (512, 512), 1)
    perm[...] = jnp.where(radius == natural, 1.0, 0.0).astype(BF16)

    def reorder(t, carry):
        invo[t] = lax.dot_general(
            perm[...], invv[t], (((1,), (1,)), ((), ())), preferred_element_type=F32
        ).astype(BF16)
        return carry

    lax.fori_loop(0, 8, reorder, 0)
    inv_out = pltpu.make_async_copy(invo, invt, i_sem.at[1])
    inv_out.start()

    own_table.wait()
    give_modes.wait()
    give_table.wait()

    right, opposite, left = (lax.rem(n + d, NARROW) for d in range(1, NARROW))

    def landed(ref, sem):
        pltpu.make_async_copy(ref, ref, sem).wait()

    def hop(src, dst, to, send_sem, recv_sem):
        pltpu.make_async_remote_copy(
            src_ref=src, dst_ref=dst, send_sem=send_sem, recv_sem=recv_sem,
            device_id=(w, to), device_id_type=MESH,
        ).start()

    def transform(k):
        landed(arecv.at[k], a_recv.at[k])
        if k + 2 < NCH:
            send_field(k + 2)

        def turn(t, carry):
            block = arecv[k, pl.ds(2 * t, 2)].reshape(16, 16, TB)
            ft[:, pl.ds(pl.multiple_of(16 * t, 16), 16), :] = jnp.swapaxes(block, 0, 1)
            return carry

        lax.fori_loop(0, 8, turn, 0)

        def two_pairs(pp, carry):
            side = pp // 2
            first = 2 * (pp % 2)
            for e in range(2):
                for kind in range(2):
                    slot = first + e + 4 * kind
                    res[e, kind] = lax.dot_general(
                        tabv[side, slot], ft[side * 8 + slot],
                        (((1,), (1,)), ((), ())), preferred_element_type=F32,
                    )

            at32 = lax.broadcasted_iota(jnp.int32, (32, 128), 0)

            def part(e, kind, block):
                rows = res[e, kind, pl.ds(pl.multiple_of(block * 32, 32), 32), :]
                m = modv[side, pl.ds(first + e + 4 * kind, 1), :]
                return jnp.where(at32 + block * 32 >= m, rows, 0.0)

            def put(pos, vals):
                for t in range(NARROW):
                    both = jnp.concatenate([v[8 * t:8 * t + 8] for v in vals], axis=0)
                    pbuf[k, t, pl.ds(pl.multiple_of(pos * 64 + pp * 16, 16), 16), :] = (
                        both.astype(BF16)
                    )

            put(0, [part(e, 1, 31) for e in range(2)])
            put(32, [part(e, 0, 31) for e in range(2)])

            def fold(v, c2):
                put(v + 1, [part(e, 0, v) + part(e, 1, 30 - v) for e in range(2)])
                return c2

            lax.fori_loop(0, 31, fold, 0)
            return carry

        lax.fori_loop(0, 4, two_pairs, 0)
        hop(pbuf.at[k, opposite, pl.ds(0, HALF)], bpass.at[k, 0], right, b_send.at[k, 0], b_recv.at[k, 0])
        hop(pbuf.at[k, opposite, pl.ds(HALF, HALF)], bpass.at[k, 1], left, b_send.at[k, 1], b_recv.at[k, 1])
        hop(pbuf.at[k, right, pl.ds(HALF, HALF)], brecv.at[k, 0, pl.ds(HALF, HALF)], right, b_send.at[k, 2], b_recv.at[k, 2])
        hop(pbuf.at[k, left, pl.ds(0, HALF)], brecv.at[k, 1, pl.ds(0, HALF)], left, b_send.at[k, 3], b_recv.at[k, 3])

    def combine(k):
        for way, (to, base) in enumerate(((right, 0), (left, HALF))):
            landed(bpass.at[k, way], b_recv.at[k, way])

            def add(t, carry):
                here = pl.ds(pl.multiple_of(base + t * 96, 32), 96)
                there = pl.ds(pl.multiple_of(t * 96, 32), 96)
                pbuf[k, to, here, :] = (
                    pbuf[k, to, here, :].astype(F32) + bpass[k, way, there, :].astype(F32)
                ).astype(BF16)
                return carry

            lax.fori_loop(0, HALF // 96, add, 0)
            half = pl.ds(base, HALF)
            hop(pbuf.at[k, to, half], brecv.at[k, way, half], to, b_send.at[k, 4 + way], b_recv.at[k, 4 + way])

    def spectral(k):
        landed(brecv.at[k, 0, pl.ds(HALF, HALF)], b_recv.at[k, 2])
        landed(brecv.at[k, 1, pl.ds(0, HALF)], b_recv.at[k, 3])
        landed(brecv.at[k, 0, pl.ds(0, HALF)], b_recv.at[k, 4])
        landed(brecv.at[k, 1, pl.ds(HALF, HALF)], b_recv.at[k, 5])

        def modes_of(kind):
            return jnp.concatenate(
                [modv[s, 4 * kind:4 * kind + 4, :] for s in range(2)], axis=0
            )

        lo_modes, hi_modes = modes_of(0), modes_of(1)
        at = lax.broadcasted_iota(jnp.int32, (8, 8, 128), 0)

        upper = lax.broadcasted_iota(jnp.int32, (8, 8, 128), 1) < 4

        def total(pos, v, m):
            rows = pl.ds(pl.multiple_of(pos * 64, 64), 64)
            vals = pbuf[k, n, rows, :].astype(F32)
            for d in range(2):
                vals = vals + brecv[k, d, rows, :].astype(F32)
            turned = jnp.swapaxes(vals.reshape(8, 8, 128), 0, 1)
            return jnp.where(at + (v * 32 + n * 8) >= m[None], turned, 0.0)

        def low(v, carry):
            csend[k, v, pl.ds(0, 64), :] = total(v + 1, v, lo_modes).reshape(64, 128).astype(BF16)
            return carry

        def high(v, carry):
            lo = total(v + 1, v, lo_modes)
            hi = total(31 - v, v, hi_modes)
            first = jnp.where(upper, lo, pltpu.roll(hi, 4, 1))
            second = jnp.where(upper, pltpu.roll(lo, 4, 1), hi)
            both = jnp.concatenate([first, second], axis=1).reshape(128, 128)
            csend[k, v] = both.astype(BF16)
            return carry

        lax.fori_loop(0, WIDE // 2, low, 0)
        lax.fori_loop(WIDE // 2, WIDE, high, 0)

        target = crecv.at[k, q, core]

        def keep(count):
            pltpu.make_async_copy(
                csend.at[k, w, pl.ds(0, count)], target.at[pl.ds(0, count)], c_recv.at[k]
            ).start()

        @pl.when(w >= WIDE // 2)
        def _():
            keep(128)

        @pl.when(w < WIDE // 2)
        def _():
            keep(64)

        def give(t, carry):
            u, c2 = t % 16, t // 16
            dy, dz = u % 4, (u // 4 + u) % 4
            to = (
                lax.rem(y + dy + core * (4 - 2 * dy), 4) * 8
                + lax.rem(z + dz + core * (4 - 2 * dz), 4) * 2
                + lax.rem(core + c2, 2)
            )

            def go(count):
                pltpu.make_async_remote_copy(
                    src_ref=csend.at[k, to, pl.ds(0, count)],
                    dst_ref=target.at[pl.ds(0, count)],
                    send_sem=c_send.at[k], recv_sem=c_recv.at[k],
                    device_id=(to, n), device_id_type=MESH,
                ).start()

            @pl.when(to >= WIDE // 2)
            def _():
                go(128)

            @pl.when(to < WIDE // 2)
            def _():
                go(64)

            return carry

        lax.fori_loop(1, WIDE, give, 0)

    def received(k):
        @pl.when(w >= WIDE // 2)
        def _():
            landed(crecv.at[k], c_recv.at[k])

        @pl.when(w < WIDE // 2)
        def _():
            landed(crecv.at[k, :, :, pl.ds(0, 64)], c_recv.at[k])

    for k in range(NCH):
        transform(k)
        if k:
            spectral(k - 1)
        combine(k)
    spectral(NCH - 1)
    for k in range(NCH):
        received(k)

    for k in range(NCH):
        landed(arecv.at[k, pl.ds(0, 15)], a_send.at[k])
        for i in range(6):
            landed(bpass.at[k, 0], b_send.at[k, i])

        @pl.when(w >= WIDE // 2)
        def _():
            landed(csend.at[k, pl.ds(0, 23)], c_send.at[k])

        @pl.when(w < WIDE // 2)
        def _():
            landed(csend.at[k, pl.ds(0, 23)], c_send.at[k])
            landed(csend.at[k, 0, pl.ds(0, 64)], c_send.at[k])
    inv_out.wait()


def solve_upper(x, inv, t):
    rows = pl.ds(pl.multiple_of(t * 16, 16), 16)
    blocks = [
        jnp.concatenate([x[2 * c + g, :, half, rows, :].reshape(CHIPS * 16, 128) for c in range(2)], axis=0)
        for half in range(2) for g in range(2)
    ]
    got = jnp.dot(jnp.concatenate(blocks, axis=1), inv[t], preferred_element_type=F32)
    return got.reshape(2, 256, 512)


def solve_lower(x, inv, t):
    rows = pl.ds(pl.multiple_of((t // 2) * 16, 16), 16)
    even = lax.broadcasted_iota(jnp.int32, (CHIPS, 8, 128), 1) * 0 + t % 2 == 0
    blocks = []
    for half in range(2):
        for g in range(2):
            both = []
            for c in range(2):
                two = x[2 * c + g, :, half, rows, :].astype(F32)
                one = jnp.where(even, two[:, :8], two[:, 8:])
                both.append(one.reshape(CHIPS * 8, 128).astype(BF16))
            blocks.append(jnp.concatenate(both, axis=0))
    got = jnp.dot(
        jnp.concatenate(blocks, axis=1), inv[t], preferred_element_type=F32
    ).reshape(2 * CHIPS, 8, 512)
    upper = lax.broadcasted_iota(jnp.int32, (2 * CHIPS, 8, 512), 1) < 4
    first = jnp.where(upper, got, 0.0)
    second = jnp.where(upper, pltpu.roll(got, 4, 1), 0.0)
    return jnp.concatenate([first, second], axis=1).reshape(2, 256, 512)


def solve_kernel(where, x, inv, solved, xv, invv, outv, x_sem, i_sem, o_sem):
    def run(rows, solve):
        copies = [
            pltpu.make_async_copy(
                x.at[k, :, half, pl.ds(0, rows)], xv.at[k, :, half, pl.ds(0, rows)],
                x_sem.at[k, half],
            )
            for k in range(NCH) for half in range(2)
        ]

        def fetch(t, carry):
            pltpu.make_async_copy(inv.at[t], invv.at[t], i_sem.at[t]).start()
            return carry

        for copy in copies:
            copy.start()
        lax.fori_loop(0, 8, fetch, 0)
        for copy in copies:
            copy.wait()

        def degree(t, carry):
            pltpu.make_async_copy(inv.at[t], invv.at[t], i_sem.at[t]).wait()
            outv[t] = solve(xv, invv, t)
            pltpu.make_async_copy(outv.at[t], solved.at[t], o_sem).start()
            return carry

        lax.fori_loop(0, 8, degree, 0)

    @pl.when(where[0] >= WIDE // 2)
    def _():
        run(128, solve_upper)

    @pl.when(where[0] < WIDE // 2)
    def _():
        run(64, solve_lower)

    pltpu.make_async_copy(outv, outv, o_sem).wait()


def per_device(field, table, inverse, modes):
    fields = field.reshape(16, 2, CHIPS, 16, TB)
    any_spec = pl.BlockSpec(memory_space=pl.ANY)
    dma = pltpu.SemaphoreType.DMA
    crecv, invt = pl.pallas_call(
        transform_kernel,
        name="transform",
        out_shape=(
            jax.ShapeDtypeStruct((NCH, CHIPS, 2, 128, 128), BF16),
            jax.ShapeDtypeStruct((8, 512, 512), BF16),
        ),
        in_specs=[any_spec, any_spec, pl.BlockSpec(memory_space=pltpu.SMEM), any_spec],
        out_specs=(any_spec, any_spec),
        scratch_shapes=[
            pltpu.VMEM((NCH, CHIPS, 8, 16, TB), BF16),
            pltpu.VMEM((2, 8, DEG, TB), BF16),
            pltpu.VMEM((2, 8, 128), jnp.int32),
            pltpu.VMEM((16, 128, TB), BF16),
            pltpu.VMEM((2, 2, DEG, 128), F32),
            pltpu.VMEM((NCH, NARROW, ROWS, 128), BF16),
            pltpu.VMEM((NCH, 2, ROWS, 128), BF16),
            pltpu.VMEM((NCH, 2, HALF, 128), BF16),
            pltpu.VMEM((NCH, WIDE, 128, 128), BF16),
            pltpu.VMEM((8, 512, 512), BF16),
            pltpu.VMEM((8, 512, 512), BF16),
            pltpu.VMEM((512, 512), BF16),
            dma((NCH,)), dma((NCH,)), dma((6,)), dma((NCH, 6)), dma((NCH, 6)),
            dma((NCH,)), dma((NCH,)), dma((2,)),
        ],
        compiler_params=pltpu.CompilerParams(
            collective_id=0, has_side_effects=True, vmem_limit_bytes=60 * 2**20
        ),
    )(fields, table, modes, inverse)
    where = lax.axis_index("wide").astype(jnp.int32).reshape(1)
    return pl.pallas_call(
        solve_kernel,
        name="solve",
        out_shape=jax.ShapeDtypeStruct((8, 2, 256, 512), F32),
        in_specs=[pl.BlockSpec(memory_space=pltpu.SMEM), any_spec, any_spec],
        out_specs=any_spec,
        scratch_shapes=[
            pltpu.VMEM((NCH, CHIPS, 2, 128, 128), BF16),
            pltpu.VMEM((8, 512, 512), BF16),
            pltpu.VMEM((8, 2, 256, 512), F32),
            dma((NCH, 2)), dma((8,)), dma(()),
        ],
        compiler_params=pltpu.CompilerParams(vmem_limit_bytes=60 * 2**20),
    )(where, crecv, invt)


def solution(mesh):
    placed = (
        P("wide", None, None, "narrow"),
        P("wide", None, "narrow"),
        P(("wide", "narrow"), None, None),
        P("wide"),
    )
    return jax.shard_map(
        per_device,
        mesh=mesh,
        in_specs=placed,
        out_specs=P(("wide", "narrow"), None, None, None),
        check_vma=False,
    )
```

```python
import functools

import jax
import jax.numpy as jnp
from jax import lax
from jax.experimental import pallas as pl
from jax.experimental.pallas import tpu as pltpu
from jax.sharding import PartitionSpec as P

MESH = pl.DeviceIdType.MESH
BF16 = jnp.bfloat16
F32 = jnp.float32

WIDE = 32
NARROW = 4
CHIPS = 16
DEG = 1024
POS = 33
ROWS = POS * 64
HALF = ROWS // 2
NCH = 4
TB = 384

PLANE = [(1, 1), (2, 2), (3, 3), (0, 1), (1, 2), (2, 3), (3, 0), (0, 2), (1, 3), (2, 0), (3, 1), (0, 3), (1, 0), (2, 1), (3, 2)]


def transform_kernel(
    field, table, modes, inverse,
    crecv, invt,
    arecv, tabv, modv, ft, res, pbuf, brecv, bpass, csend, invv, invo, perm,
    a_send, a_recv, t_sem, b_send, b_recv, c_send, c_recv, i_sem,
):
    w = lax.axis_index("wide")
    n = lax.axis_index("narrow")
    q = w // 2
    core = w % 2
    y = q // 4
    z = q % 4
    sib = w + 1 - 2 * core

    own_table = pltpu.make_async_copy(table, tabv.at[core], t_sem.at[0])
    own_table.start()
    for i in range(8):
        modv[core, i, :] = jnp.full((128,), modes[i], jnp.int32)
    inv_in = pltpu.make_async_copy(inverse, invv, i_sem.at[0])
    inv_in.start()
    for k in range(NCH):
        pltpu.make_async_copy(
            field.at[pl.ds(8 * (k % 2), 8), k // 2, q], arecv.at[k, q], a_recv.at[k]
        ).start()

    barrier = pltpu.get_barrier_semaphore()

    def greet(t, carry):
        pl.semaphore_signal(
            barrier, inc=1, device_id=(lax.rem(w + t, WIDE), n), device_id_type=MESH
        )
        return carry

    lax.fori_loop(1, WIDE, greet, 0)
    for d in range(1, NARROW):
        pl.semaphore_signal(
            barrier, inc=1, device_id=(w, lax.rem(n + d, NARROW)), device_id_type=MESH
        )
    pl.semaphore_wait(barrier, WIDE - 1 + NARROW - 1)

    def send_field(k):
        for dy, dz in PLANE:
            peer = lax.rem(y + dy + core * (4 - 2 * dy), 4) * 4 + lax.rem(z + dz + core * (4 - 2 * dz), 4)
            pltpu.make_async_remote_copy(
                src_ref=field.at[pl.ds(8 * (k % 2), 8), k // 2, peer],
                dst_ref=arecv.at[k, q],
                send_sem=a_send.at[k],
                recv_sem=a_recv.at[k],
                device_id=(peer * 2 + core, n),
                device_id_type=MESH,
            ).start()

    give_modes = pltpu.make_async_remote_copy(
        src_ref=modv.at[core], dst_ref=modv.at[core], send_sem=t_sem.at[2],
        recv_sem=t_sem.at[3], device_id=(sib, n), device_id_type=MESH,
    )
    give_modes.start()
    give_table = pltpu.make_async_remote_copy(
        src_ref=table, dst_ref=tabv.at[core], send_sem=t_sem.at[4],
        recv_sem=t_sem.at[5], device_id=(sib, n), device_id_type=MESH,
    )
    send_field(0)
    give_table.start()
    send_field(1)

    inv_in.wait()
    arrive = lax.broadcasted_iota(jnp.int32, (512, 512), 0)
    natural = (
        ((arrive // 8) % 16) * 32 + (arrive // 256) * 16 + ((arrive // 128) % 2) * 8 + arrive % 8
    )
    radius = lax.broadcasted_iota(jnp.int32, (512, 512), 1)
    perm[...] = jnp.where(radius == natural, 1.0, 0.0).astype(BF16)

    def reorder(t, carry):
        invo[t] = lax.dot_general(
            perm[...], invv[t], (((1,), (1,)), ((), ())), preferred_element_type=F32
        ).astype(BF16)
        return carry

    lax.fori_loop(0, 8, reorder, 0)
    inv_out = pltpu.make_async_copy(invo, invt, i_sem.at[1])
    inv_out.start()

    own_table.wait()
    give_modes.wait()
    give_table.wait()

    right, opposite, left = (lax.rem(n + d, NARROW) for d in range(1, NARROW))

    def landed(ref, sem):
        pltpu.make_async_copy(ref, ref, sem).wait()

    def hop(src, dst, to, send_sem, recv_sem):
        pltpu.make_async_remote_copy(
            src_ref=src, dst_ref=dst, send_sem=send_sem, recv_sem=recv_sem,
            device_id=(w, to), device_id_type=MESH,
        ).start()

    def transform(k):
        landed(arecv.at[k], a_recv.at[k])
        if k + 2 < NCH:
            send_field(k + 2)

        def turn(t, carry):
            block = arecv[k, pl.ds(2 * t, 2)].reshape(16, 16, TB)
            ft[:, pl.ds(pl.multiple_of(16 * t, 16), 16), :] = jnp.swapaxes(block, 0, 1)
            return carry

        lax.fori_loop(0, 8, turn, 0)

        def two_pairs(pp, carry):
            side = pp // 2
            first = 2 * (pp % 2)
            for e in range(2):
                for kind in range(2):
                    slot = first + e + 4 * kind
                    res[e, kind] = lax.dot_general(
                        tabv[side, slot], ft[side * 8 + slot],
                        (((1,), (1,)), ((), ())), preferred_element_type=F32,
                    )

            at32 = lax.broadcasted_iota(jnp.int32, (32, 128), 0)

            def part(e, kind, block):
                rows = res[e, kind, pl.ds(pl.multiple_of(block * 32, 32), 32), :]
                m = modv[side, pl.ds(first + e + 4 * kind, 1), :]
                return jnp.where(at32 + block * 32 >= m, rows, 0.0)

            def put(pos, vals):
                for t in range(NARROW):
                    both = jnp.concatenate([v[8 * t:8 * t + 8] for v in vals], axis=0)
                    pbuf[k, t, pl.ds(pl.multiple_of(pos * 64 + pp * 16, 16), 16), :] = (
                        both.astype(BF16)
                    )

            put(0, [part(e, 1, 31) for e in range(2)])
            put(32, [part(e, 0, 31) for e in range(2)])

            def fold(v, c2):
                put(v + 1, [part(e, 0, v) + part(e, 1, 30 - v) for e in range(2)])
                return c2

            lax.fori_loop(0, 31, fold, 0)
            return carry

        lax.fori_loop(0, 4, two_pairs, 0)
        hop(pbuf.at[k, opposite, pl.ds(0, HALF)], bpass.at[k, 0], right, b_send.at[k, 0], b_recv.at[k, 0])
        hop(pbuf.at[k, opposite, pl.ds(HALF, HALF)], bpass.at[k, 1], left, b_send.at[k, 1], b_recv.at[k, 1])
        hop(pbuf.at[k, right, pl.ds(HALF, HALF)], brecv.at[k, 0, pl.ds(HALF, HALF)], right, b_send.at[k, 2], b_recv.at[k, 2])
        hop(pbuf.at[k, left, pl.ds(0, HALF)], brecv.at[k, 1, pl.ds(0, HALF)], left, b_send.at[k, 3], b_recv.at[k, 3])

    def combine(k):
        for way, (to, base) in enumerate(((right, 0), (left, HALF))):
            landed(bpass.at[k, way], b_recv.at[k, way])

            def add(t, carry):
                here = pl.ds(pl.multiple_of(base + t * 96, 32), 96)
                there = pl.ds(pl.multiple_of(t * 96, 32), 96)
                pbuf[k, to, here, :] = (
                    pbuf[k, to, here, :].astype(F32) + bpass[k, way, there, :].astype(F32)
                ).astype(BF16)
                return carry

            lax.fori_loop(0, HALF // 96, add, 0)
            half = pl.ds(base, HALF)
            hop(pbuf.at[k, to, half], brecv.at[k, way, half], to, b_send.at[k, 4 + way], b_recv.at[k, 4 + way])

    def spectral(k):
        landed(brecv.at[k, 0, pl.ds(HALF, HALF)], b_recv.at[k, 2])
        landed(brecv.at[k, 1, pl.ds(0, HALF)], b_recv.at[k, 3])
        landed(brecv.at[k, 0, pl.ds(0, HALF)], b_recv.at[k, 4])
        landed(brecv.at[k, 1, pl.ds(HALF, HALF)], b_recv.at[k, 5])

        def modes_of(kind):
            return jnp.concatenate(
                [modv[s, 4 * kind:4 * kind + 4, :] for s in range(2)], axis=0
            )

        lo_modes, hi_modes = modes_of(0), modes_of(1)
        at = lax.broadcasted_iota(jnp.int32, (8, 8, 128), 0)

        upper = lax.broadcasted_iota(jnp.int32, (8, 8, 128), 1) < 4

        def total(pos, v, m):
            rows = pl.ds(pl.multiple_of(pos * 64, 64), 64)
            vals = pbuf[k, n, rows, :].astype(F32)
            for d in range(2):
                vals = vals + brecv[k, d, rows, :].astype(F32)
            turned = jnp.swapaxes(vals.reshape(8, 8, 128), 0, 1)
            return jnp.where(at + (v * 32 + n * 8) >= m[None], turned, 0.0)

        def low(v, carry):
            lo = total(v + 1, v, lo_modes).reshape(4, 16, 128)
            csend[k, v, :, pl.ds(0, 16), :] = lo.astype(BF16)
            return carry

        def high(v, carry):
            lo = total(v + 1, v, lo_modes)
            hi = total(31 - v, v, hi_modes)
            first = jnp.where(upper, lo, pltpu.roll(hi, 4, 1))
            second = jnp.where(upper, pltpu.roll(lo, 4, 1), hi)
            both = jnp.concatenate([first, second], axis=1).reshape(4, 32, 128)
            csend[k, v] = both.astype(BF16)
            return carry

        lax.fori_loop(0, WIDE // 2, low, 0)
        lax.fori_loop(WIDE // 2, WIDE, high, 0)

        target = crecv.at[:, k, q, core]

        def keep(count):
            pltpu.make_async_copy(
                csend.at[k, w, :, pl.ds(0, count)], target.at[:, pl.ds(0, count)], c_recv.at[k]
            ).start()

        @pl.when(w >= WIDE // 2)
        def _():
            keep(32)

        @pl.when(w < WIDE // 2)
        def _():
            keep(16)

        def give(t, carry):
            u, c2 = t % 16, t // 16
            dy, dz = u % 4, (u // 4 + u) % 4
            to = (
                lax.rem(y + dy + core * (4 - 2 * dy), 4) * 8
                + lax.rem(z + dz + core * (4 - 2 * dz), 4) * 2
                + lax.rem(core + c2, 2)
            )

            def go(count):
                pltpu.make_async_remote_copy(
                    src_ref=csend.at[k, to, :, pl.ds(0, count)],
                    dst_ref=target.at[:, pl.ds(0, count)],
                    send_sem=c_send.at[k], recv_sem=c_recv.at[k],
                    device_id=(to, n), device_id_type=MESH,
                ).start()

            @pl.when(to >= WIDE // 2)
            def _():
                go(32)

            @pl.when(to < WIDE // 2)
            def _():
                go(16)

            return carry

        lax.fori_loop(1, WIDE, give, 0)

    def received(k):
        @pl.when(w >= WIDE // 2)
        def _():
            landed(crecv.at[:, k], c_recv.at[k])

        @pl.when(w < WIDE // 2)
        def _():
            landed(crecv.at[:, k, :, :, pl.ds(0, 16)], c_recv.at[k])

    for k in range(NCH):
        transform(k)
        if k:
            spectral(k - 1)
        combine(k)
    spectral(NCH - 1)
    for k in range(NCH):
        received(k)

    for k in range(NCH):
        landed(arecv.at[k, pl.ds(0, 15)], a_send.at[k])
        for i in range(6):
            landed(bpass.at[k, 0], b_send.at[k, i])

        @pl.when(w >= WIDE // 2)
        def _():
            landed(csend.at[k, pl.ds(0, 23)], c_send.at[k])

        @pl.when(w < WIDE // 2)
        def _():
            landed(csend.at[k, pl.ds(0, 23)], c_send.at[k])
            landed(csend.at[k, 0, :, pl.ds(0, 16)], c_send.at[k])
    inv_out.wait()


def solve_upper(x, inv, pair, e):
    blocks = [
        jnp.concatenate(
            [
                x[pair, 2 * c + g, :, half, 16 * e:16 * e + 16, :].reshape(CHIPS * 16, 128)
                for c in range(2)
            ],
            axis=0,
        )
        for half in range(2) for g in range(2)
    ]
    got = jnp.dot(
        jnp.concatenate(blocks, axis=1), inv[2 * pair + e], preferred_element_type=F32
    )
    return got.reshape(2, 256, 512)


def solve_lower(x, inv, pair, e):
    blocks = []
    for half in range(2):
        for g in range(2):
            both = []
            for c in range(2):
                two = x[pair, 2 * c + g, :, half, 0:16, :].astype(F32)
                both.append(two[:, 8 * e:8 * e + 8].reshape(CHIPS * 8, 128).astype(BF16))
            blocks.append(jnp.concatenate(both, axis=0))
    got = jnp.dot(
        jnp.concatenate(blocks, axis=1), inv[2 * pair + e], preferred_element_type=F32
    ).reshape(2 * CHIPS, 8, 512)
    upper = lax.broadcasted_iota(jnp.int32, (2 * CHIPS, 8, 512), 1) < 4
    first = jnp.where(upper, got, 0.0)
    second = jnp.where(upper, pltpu.roll(got, 4, 1), 0.0)
    return jnp.concatenate([first, second], axis=1).reshape(2, 256, 512)


def solve_kernel(where, x, inv, solved, xv, invv, outv, x_sem, i_sem, o_sem):
    def run(rows, solve):
        def rows_of(pair):
            part = (pair, slice(None), slice(None), slice(None), pl.ds(0, rows))
            return pltpu.make_async_copy(x.at[part], xv.at[part], x_sem.at[pair])

        def inverse_of(t):
            return pltpu.make_async_copy(inv.at[t], invv.at[t], i_sem.at[t])

        def fetch(pair, carry):
            rows_of(pair).start()
            inverse_of(2 * pair).start()
            inverse_of(2 * pair + 1).start()
            return carry

        lax.fori_loop(0, 4, fetch, 0)

        def degrees(pair, carry):
            rows_of(pair).wait()
            for e in range(2):
                t = 2 * pair + e
                inverse_of(t).wait()
                outv[t] = solve(xv, invv, pair, e)
                pltpu.make_async_copy(outv.at[t], solved.at[t], o_sem).start()
            return carry

        lax.fori_loop(0, 4, degrees, 0)

    @pl.when(where[0] >= WIDE // 2)
    def _():
        run(32, solve_upper)

    @pl.when(where[0] < WIDE // 2)
    def _():
        run(16, solve_lower)

    pltpu.make_async_copy(outv, outv, o_sem).wait()


def per_device(field, table, inverse, modes):
    fields = field.reshape(16, 2, CHIPS, 16, TB)
    any_spec = pl.BlockSpec(memory_space=pl.ANY)
    dma = pltpu.SemaphoreType.DMA
    crecv, invt = pl.pallas_call(
        transform_kernel,
        name="transform",
        out_shape=(
            jax.ShapeDtypeStruct((4, NCH, CHIPS, 2, 32, 128), BF16),
            jax.ShapeDtypeStruct((8, 512, 512), BF16),
        ),
        in_specs=[any_spec, any_spec, pl.BlockSpec(memory_space=pltpu.SMEM), any_spec],
        out_specs=(any_spec, any_spec),
        scratch_shapes=[
            pltpu.VMEM((NCH, CHIPS, 8, 16, TB), BF16),
            pltpu.VMEM((2, 8, DEG, TB), BF16),
            pltpu.VMEM((2, 8, 128), jnp.int32),
            pltpu.VMEM((16, 128, TB), BF16),
            pltpu.VMEM((2, 2, DEG, 128), F32),
            pltpu.VMEM((NCH, NARROW, ROWS, 128), BF16),
            pltpu.VMEM((NCH, 2, ROWS, 128), BF16),
            pltpu.VMEM((NCH, 2, HALF, 128), BF16),
            pltpu.VMEM((NCH, WIDE, 4, 32, 128), BF16),
            pltpu.VMEM((8, 512, 512), BF16),
            pltpu.VMEM((8, 512, 512), BF16),
            pltpu.VMEM((512, 512), BF16),
            dma((NCH,)), dma((NCH,)), dma((6,)), dma((NCH, 6)), dma((NCH, 6)),
            dma((NCH,)), dma((NCH,)), dma((2,)),
        ],
        compiler_params=pltpu.CompilerParams(
            collective_id=0, has_side_effects=True, vmem_limit_bytes=60 * 2**20
        ),
    )(fields, table, modes, inverse)
    where = lax.axis_index("wide").astype(jnp.int32).reshape(1)
    return pl.pallas_call(
        solve_kernel,
        name="solve",
        out_shape=jax.ShapeDtypeStruct((8, 2, 256, 512), F32),
        in_specs=[pl.BlockSpec(memory_space=pltpu.SMEM), any_spec, any_spec],
        out_specs=any_spec,
        scratch_shapes=[
            pltpu.VMEM((4, NCH, CHIPS, 2, 32, 128), BF16),
            pltpu.VMEM((8, 512, 512), BF16),
            pltpu.VMEM((8, 2, 256, 512), F32),
            dma((4,)), dma((8,)), dma(()),
        ],
        compiler_params=pltpu.CompilerParams(vmem_limit_bytes=60 * 2**20),
    )(where, crecv, invt)


def solution(mesh):
    placed = (
        P("wide", None, None, "narrow"),
        P("wide", None, "narrow"),
        P(("wide", "narrow"), None, None),
        P("wide"),
    )
    return jax.shard_map(
        per_device,
        mesh=mesh,
        in_specs=placed,
        out_specs=P(("wide", "narrow"), None, None, None),
        check_vma=False,
    )
```

```python
import functools

import jax
import jax.numpy as jnp
from jax import lax
from jax.experimental import pallas as pl
from jax.experimental.pallas import tpu as pltpu
from jax.sharding import PartitionSpec as P

MESH = pl.DeviceIdType.MESH
BF16 = jnp.bfloat16
F32 = jnp.float32

WIDE = 32
NARROW = 4
CHIPS = 16
DEG = 1024
POS = 33
ROWS = POS * 64
HALF = ROWS // 2
NCH = 4
TB = 384

PLANE = [(1, 1), (2, 2), (3, 3), (0, 1), (1, 2), (2, 3), (3, 0), (0, 2), (1, 3), (2, 0), (3, 1), (0, 3), (1, 0), (2, 1), (3, 2)]


def transform_kernel(
    field, table, modes, inverse,
    crecv, invt,
    arecv, tabv, modv, ft, res, pbuf, brecv, bpass, csend, invv, invo, perm,
    a_send, a_recv, t_sem, b_send, b_recv, c_send, c_recv, i_sem,
):
    w = lax.axis_index("wide")
    n = lax.axis_index("narrow")
    q = w // 2
    core = w % 2
    y = q // 4
    z = q % 4
    sib = w + 1 - 2 * core

    own_table = pltpu.make_async_copy(table, tabv.at[core], t_sem.at[0])
    own_table.start()
    for i in range(8):
        modv[core, i, :] = jnp.full((128,), modes[i], jnp.int32)
    inv_in = pltpu.make_async_copy(inverse, invv, i_sem.at[0])
    inv_in.start()
    for k in range(NCH):
        pltpu.make_async_copy(
            field.at[pl.ds(8 * (k % 2), 8), k // 2, q], arecv.at[k, q], a_recv.at[k]
        ).start()

    barrier = pltpu.get_barrier_semaphore()

    def greet(t, carry):
        pl.semaphore_signal(
            barrier, inc=1, device_id=(lax.rem(w + t, WIDE), n), device_id_type=MESH
        )
        return carry

    lax.fori_loop(1, WIDE, greet, 0)
    for d in range(1, NARROW):
        pl.semaphore_signal(
            barrier, inc=1, device_id=(w, lax.rem(n + d, NARROW)), device_id_type=MESH
        )
    pl.semaphore_wait(barrier, WIDE - 1 + NARROW - 1)

    def send_field(k):
        for dy, dz in PLANE:
            peer = lax.rem(y + dy + core * (4 - 2 * dy), 4) * 4 + lax.rem(z + dz + core * (4 - 2 * dz), 4)
            pltpu.make_async_remote_copy(
                src_ref=field.at[pl.ds(8 * (k % 2), 8), k // 2, peer],
                dst_ref=arecv.at[k, q],
                send_sem=a_send.at[k],
                recv_sem=a_recv.at[k],
                device_id=(peer * 2 + core, n),
                device_id_type=MESH,
            ).start()

    give_modes = pltpu.make_async_remote_copy(
        src_ref=modv.at[core], dst_ref=modv.at[core], send_sem=t_sem.at[2],
        recv_sem=t_sem.at[3], device_id=(sib, n), device_id_type=MESH,
    )
    give_modes.start()
    give_table = pltpu.make_async_remote_copy(
        src_ref=table, dst_ref=tabv.at[core], send_sem=t_sem.at[4],
        recv_sem=t_sem.at[5], device_id=(sib, n), device_id_type=MESH,
    )
    send_field(0)
    give_table.start()
    send_field(1)

    inv_in.wait()
    arrive = lax.broadcasted_iota(jnp.int32, (512, 512), 0)
    natural = (
        ((arrive // 8) % 16) * 32 + (arrive // 256) * 16 + ((arrive // 128) % 2) * 8 + arrive % 8
    )
    radius = lax.broadcasted_iota(jnp.int32, (512, 512), 1)
    perm[...] = jnp.where(radius == natural, 1.0, 0.0).astype(BF16)

    def reorder(t, carry):
        invo[t] = lax.dot_general(
            perm[...], invv[t], (((1,), (1,)), ((), ())), preferred_element_type=F32
        ).astype(BF16)
        return carry

    lax.fori_loop(0, 8, reorder, 0)
    inv_out = pltpu.make_async_copy(invo, invt, i_sem.at[1])
    inv_out.start()

    own_table.wait()
    give_modes.wait()
    give_table.wait()

    right, opposite, left = (lax.rem(n + d, NARROW) for d in range(1, NARROW))

    def landed(ref, sem):
        pltpu.make_async_copy(ref, ref, sem).wait()

    def hop(src, dst, to, send_sem, recv_sem):
        pltpu.make_async_remote_copy(
            src_ref=src, dst_ref=dst, send_sem=send_sem, recv_sem=recv_sem,
            device_id=(w, to), device_id_type=MESH,
        ).start()

    def transform(k):
        landed(arecv.at[k], a_recv.at[k])
        if k + 2 < NCH:
            send_field(k + 2)

        def turn(t, carry):
            block = arecv[k, pl.ds(2 * t, 2)].reshape(16, 16, TB)
            ft[:, pl.ds(pl.multiple_of(16 * t, 16), 16), :] = jnp.swapaxes(block, 0, 1)
            return carry

        lax.fori_loop(0, 8, turn, 0)

        def two_pairs(pp, carry):
            side = pp // 2
            first = 2 * (pp % 2)
            for e in range(2):
                for kind in range(2):
                    slot = first + e + 4 * kind
                    res[e, kind] = lax.dot_general(
                        tabv[side, slot], ft[side * 8 + slot],
                        (((1,), (1,)), ((), ())), preferred_element_type=F32,
                    )

            at32 = lax.broadcasted_iota(jnp.int32, (32, 128), 0)

            def part(e, kind, block):
                rows = res[e, kind, pl.ds(pl.multiple_of(block * 32, 32), 32), :]
                m = modv[side, pl.ds(first + e + 4 * kind, 1), :]
                return jnp.where(at32 + block * 32 >= m, rows, 0.0)

            def put(pos, vals):
                for t in range(NARROW):
                    both = jnp.concatenate([v[8 * t:8 * t + 8] for v in vals], axis=0)
                    pbuf[k, t, pl.ds(pl.multiple_of(pos * 64 + pp * 16, 16), 16), :] = (
                        both.astype(BF16)
                    )

            put(0, [part(e, 1, 31) for e in range(2)])
            put(32, [part(e, 0, 31) for e in range(2)])

            def fold(v, c2):
                put(v + 1, [part(e, 0, v) + part(e, 1, 30 - v) for e in range(2)])
                return c2

            lax.fori_loop(0, 31, fold, 0)
            return carry

        lax.fori_loop(0, 4, two_pairs, 0)
        hop(pbuf.at[k, opposite, pl.ds(0, HALF)], bpass.at[k, 0], right, b_send.at[k, 0], b_recv.at[k, 0])
        hop(pbuf.at[k, opposite, pl.ds(HALF, HALF)], bpass.at[k, 1], left, b_send.at[k, 1], b_recv.at[k, 1])
        hop(pbuf.at[k, right, pl.ds(HALF, HALF)], brecv.at[k, 0, pl.ds(HALF, HALF)], right, b_send.at[k, 2], b_recv.at[k, 2])
        hop(pbuf.at[k, left, pl.ds(0, HALF)], brecv.at[k, 1, pl.ds(0, HALF)], left, b_send.at[k, 3], b_recv.at[k, 3])

    def combine(k):
        for way, (to, base) in enumerate(((right, 0), (left, HALF))):
            landed(bpass.at[k, way], b_recv.at[k, way])

            def add(t, carry):
                here = pl.ds(pl.multiple_of(base + t * 96, 32), 96)
                there = pl.ds(pl.multiple_of(t * 96, 32), 96)
                pbuf[k, to, here, :] = (
                    pbuf[k, to, here, :].astype(F32) + bpass[k, way, there, :].astype(F32)
                ).astype(BF16)
                return carry

            lax.fori_loop(0, HALF // 96, add, 0)
            half = pl.ds(base, HALF)
            hop(pbuf.at[k, to, half], brecv.at[k, way, half], to, b_send.at[k, 4 + way], b_recv.at[k, 4 + way])

    def spectral(k):
        landed(brecv.at[k, 0, pl.ds(HALF, HALF)], b_recv.at[k, 2])
        landed(brecv.at[k, 1, pl.ds(0, HALF)], b_recv.at[k, 3])
        landed(brecv.at[k, 0, pl.ds(0, HALF)], b_recv.at[k, 4])
        landed(brecv.at[k, 1, pl.ds(HALF, HALF)], b_recv.at[k, 5])

        def modes_of(kind):
            return jnp.concatenate(
                [modv[s, 4 * kind:4 * kind + 4, :] for s in range(2)], axis=0
            )

        lo_modes, hi_modes = modes_of(0), modes_of(1)
        at = lax.broadcasted_iota(jnp.int32, (8, 8, 128), 0)

        upper = lax.broadcasted_iota(jnp.int32, (8, 8, 128), 1) < 4

        def total(pos, v, m):
            rows = pl.ds(pl.multiple_of(pos * 64, 64), 64)
            vals = pbuf[k, n, rows, :].astype(F32)
            for d in range(2):
                vals = vals + brecv[k, d, rows, :].astype(F32)
            turned = jnp.swapaxes(vals.reshape(8, 8, 128), 0, 1)
            return jnp.where(at + (v * 32 + n * 8) >= m[None], turned, 0.0)

        def low(v, carry):
            lo = total(v + 1, v, lo_modes).reshape(4, 16, 128)
            csend[k, v, :, pl.ds(0, 16), :] = lo.astype(BF16)
            return carry

        def high(v, carry):
            lo = total(v + 1, v, lo_modes)
            hi = total(31 - v, v, hi_modes)
            first = jnp.where(upper, lo, pltpu.roll(hi, 4, 1))
            second = jnp.where(upper, pltpu.roll(lo, 4, 1), hi)
            both = jnp.concatenate([first, second], axis=1).reshape(4, 32, 128)
            csend[k, v] = both.astype(BF16)
            return carry

        lax.fori_loop(0, WIDE // 2, low, 0)
        lax.fori_loop(WIDE // 2, WIDE, high, 0)

        target = crecv.at[:, k, q, core]

        def keep(count):
            pltpu.make_async_copy(
                csend.at[k, w, :, pl.ds(0, count)], target.at[:, pl.ds(0, count)], c_recv.at[k]
            ).start()

        @pl.when(w >= WIDE // 2)
        def _():
            keep(32)

        @pl.when(w < WIDE // 2)
        def _():
            keep(16)

        def give(t, carry):
            u = lax.rem(t, 16)
            to = (
                16 - 16 * (t // 16) + 8 * lax.rem(y + u, 2) + 2 * lax.rem(z + u // 2, 4)
                + lax.rem(core + u // 8, 2)
            )

            def go(count):
                pltpu.make_async_remote_copy(
                    src_ref=csend.at[k, to, :, pl.ds(0, count)],
                    dst_ref=target.at[:, pl.ds(0, count)],
                    send_sem=c_send.at[k], recv_sem=c_recv.at[k],
                    device_id=(to, n), device_id_type=MESH,
                ).start()

            @pl.when((to >= WIDE // 2) & (to != w))
            def _():
                go(32)

            @pl.when((to < WIDE // 2) & (to != w))
            def _():
                go(16)

            return carry

        lax.fori_loop(0, WIDE, give, 0)

    def received(k):
        @pl.when(w >= WIDE // 2)
        def _():
            landed(crecv.at[:, k], c_recv.at[k])

        @pl.when(w < WIDE // 2)
        def _():
            landed(crecv.at[:, k, :, :, pl.ds(0, 16)], c_recv.at[k])

    for k in range(NCH):
        transform(k)
        if k:
            spectral(k - 1)
        combine(k)
    spectral(NCH - 1)
    for k in range(NCH):
        received(k)

    for k in range(NCH):
        landed(arecv.at[k, pl.ds(0, 15)], a_send.at[k])
        for i in range(6):
            landed(bpass.at[k, 0], b_send.at[k, i])

        @pl.when(w >= WIDE // 2)
        def _():
            landed(csend.at[k, pl.ds(0, 23)], c_send.at[k])

        @pl.when(w < WIDE // 2)
        def _():
            landed(csend.at[k, pl.ds(0, 23)], c_send.at[k])
            landed(csend.at[k, 0, :, pl.ds(0, 16)], c_send.at[k])
    inv_out.wait()


def solve_upper(x, inv, pair, e):
    blocks = [
        jnp.concatenate(
            [
                x[pair, 2 * c + g, :, half, 16 * e:16 * e + 16, :].reshape(CHIPS * 16, 128)
                for c in range(2)
            ],
            axis=0,
        )
        for half in range(2) for g in range(2)
    ]
    got = jnp.dot(
        jnp.concatenate(blocks, axis=1), inv[2 * pair + e], preferred_element_type=F32
    )
    return got.reshape(2, 256, 512)


def solve_lower(x, inv, pair, e):
    blocks = []
    for half in range(2):
        for g in range(2):
            both = []
            for c in range(2):
                two = x[pair, 2 * c + g, :, half, 0:16, :].astype(F32)
                both.append(two[:, 8 * e:8 * e + 8].reshape(CHIPS * 8, 128).astype(BF16))
            blocks.append(jnp.concatenate(both, axis=0))
    got = jnp.dot(
        jnp.concatenate(blocks, axis=1), inv[2 * pair + e], preferred_element_type=F32
    ).reshape(2 * CHIPS, 8, 512)
    upper = lax.broadcasted_iota(jnp.int32, (2 * CHIPS, 8, 512), 1) < 4
    first = jnp.where(upper, got, 0.0)
    second = jnp.where(upper, pltpu.roll(got, 4, 1), 0.0)
    return jnp.concatenate([first, second], axis=1).reshape(2, 256, 512)


def solve_kernel(where, x, inv, solved, xv, invv, outv, x_sem, i_sem, o_sem):
    def run(rows, solve):
        def rows_of(pair):
            part = (pair, slice(None), slice(None), slice(None), pl.ds(0, rows))
            return pltpu.make_async_copy(x.at[part], xv.at[part], x_sem.at[pair])

        def inverse_of(t):
            return pltpu.make_async_copy(inv.at[t], invv.at[t], i_sem.at[t])

        def fetch(pair, carry):
            rows_of(pair).start()
            inverse_of(2 * pair).start()
            inverse_of(2 * pair + 1).start()
            return carry

        lax.fori_loop(0, 4, fetch, 0)

        def degrees(pair, carry):
            rows_of(pair).wait()
            for e in range(2):
                t = 2 * pair + e
                inverse_of(t).wait()
                outv[t] = solve(xv, invv, pair, e)
                for c in range(2):
                    pltpu.make_async_copy(outv.at[t, c], solved.at[t, c], o_sem).start()
            return carry

        lax.fori_loop(0, 4, degrees, 0)

    @pl.when(where[0] >= WIDE // 2)
    def _():
        run(32, solve_upper)

    @pl.when(where[0] < WIDE // 2)
    def _():
        run(16, solve_lower)

    pltpu.make_async_copy(outv, outv, o_sem).wait()


def per_device(field, table, inverse, modes):
    fields = field.reshape(16, 2, CHIPS, 16, TB)
    any_spec = pl.BlockSpec(memory_space=pl.ANY)
    dma = pltpu.SemaphoreType.DMA
    crecv, invt = pl.pallas_call(
        transform_kernel,
        name="transform",
        out_shape=(
            jax.ShapeDtypeStruct((4, NCH, CHIPS, 2, 32, 128), BF16),
            jax.ShapeDtypeStruct((8, 512, 512), BF16),
        ),
        in_specs=[any_spec, any_spec, pl.BlockSpec(memory_space=pltpu.SMEM), any_spec],
        out_specs=(any_spec, any_spec),
        scratch_shapes=[
            pltpu.VMEM((NCH, CHIPS, 8, 16, TB), BF16),
            pltpu.VMEM((2, 8, DEG, TB), BF16),
            pltpu.VMEM((2, 8, 128), jnp.int32),
            pltpu.VMEM((16, 128, TB), BF16),
            pltpu.VMEM((2, 2, DEG, 128), F32),
            pltpu.VMEM((NCH, NARROW, ROWS, 128), BF16),
            pltpu.VMEM((NCH, 2, ROWS, 128), BF16),
            pltpu.VMEM((NCH, 2, HALF, 128), BF16),
            pltpu.VMEM((NCH, WIDE, 4, 32, 128), BF16),
            pltpu.VMEM((8, 512, 512), BF16),
            pltpu.VMEM((8, 512, 512), BF16),
            pltpu.VMEM((512, 512), BF16),
            dma((NCH,)), dma((NCH,)), dma((6,)), dma((NCH, 6)), dma((NCH, 6)),
            dma((NCH,)), dma((NCH,)), dma((2,)),
        ],
        compiler_params=pltpu.CompilerParams(
            collective_id=0, has_side_effects=True, vmem_limit_bytes=60 * 2**20
        ),
    )(fields, table, modes, inverse)
    where = lax.axis_index("wide").astype(jnp.int32).reshape(1)
    return pl.pallas_call(
        solve_kernel,
        name="solve",
        out_shape=jax.ShapeDtypeStruct((8, 2, 256, 512), F32),
        in_specs=[pl.BlockSpec(memory_space=pltpu.SMEM), any_spec, any_spec],
        out_specs=any_spec,
        scratch_shapes=[
            pltpu.VMEM((4, NCH, CHIPS, 2, 32, 128), BF16),
            pltpu.VMEM((8, 512, 512), BF16),
            pltpu.VMEM((8, 2, 256, 512), F32),
            dma((4,)), dma((8,)), dma(()),
        ],
        compiler_params=pltpu.CompilerParams(vmem_limit_bytes=60 * 2**20),
    )(where, crecv, invt)


def solution(mesh):
    placed = (
        P("wide", None, None, "narrow"),
        P("wide", None, "narrow"),
        P(("wide", "narrow"), None, None),
        P("wide"),
    )
    return jax.shard_map(
        per_device,
        mesh=mesh,
        in_specs=placed,
        out_specs=P(("wide", "narrow"), None, None, None),
        check_vma=False,
    )
```

```python
import functools

import jax
import jax.numpy as jnp
from jax import lax
from jax.experimental import pallas as pl
from jax.experimental.pallas import tpu as pltpu
from jax.sharding import PartitionSpec as P

MESH = pl.DeviceIdType.MESH
BF16 = jnp.bfloat16
F32 = jnp.float32

WIDE = 32
NARROW = 4
CHIPS = 16
DEG = 1024
POS = 33
ROWS = POS * 64
HALF = ROWS // 2
NCH = 4
TB = 384

PLANE = [(1, 1), (2, 2), (3, 3), (0, 1), (1, 2), (2, 3), (3, 0), (0, 2), (1, 3), (2, 0), (3, 1), (0, 3), (1, 0), (2, 1), (3, 2)]


def transform_kernel(
    field, table, modes, inverse,
    crecv, invt,
    arecv, tabv, modv, ft, res, pbuf, brecv, bpass, csend, invv, invo, perm,
    a_send, a_recv, t_sem, b_send, b_recv, c_send, c_recv, i_sem,
):
    w = lax.axis_index("wide")
    n = lax.axis_index("narrow")
    q = w // 2
    core = w % 2
    y = q // 4
    z = q % 4
    sib = w + 1 - 2 * core

    barrier = pltpu.get_barrier_semaphore()

    def greet(t, carry):
        pl.semaphore_signal(
            barrier, inc=1, device_id=(lax.rem(w + t, WIDE), n), device_id_type=MESH
        )
        return carry

    lax.fori_loop(1, WIDE, greet, 0)
    for d in range(1, NARROW):
        pl.semaphore_signal(
            barrier, inc=1, device_id=(w, lax.rem(n + d, NARROW)), device_id_type=MESH
        )
    own_table = pltpu.make_async_copy(table, tabv.at[core], t_sem.at[0])
    own_table.start()
    for i in range(8):
        modv[core, i, :] = jnp.full((128,), modes[i], jnp.int32)
    inv_in = pltpu.make_async_copy(inverse, invv, i_sem.at[0])
    inv_in.start()
    for k in range(NCH):
        pltpu.make_async_copy(
            field.at[pl.ds(8 * (k % 2), 8), k // 2, q], arecv.at[k, q], a_recv.at[k]
        ).start()

    pl.semaphore_wait(barrier, WIDE - 1 + NARROW - 1)

    def send_field(k):
        for dy, dz in PLANE:
            peer = lax.rem(y + dy + core * (4 - 2 * dy), 4) * 4 + lax.rem(z + dz + core * (4 - 2 * dz), 4)
            pltpu.make_async_remote_copy(
                src_ref=field.at[pl.ds(8 * (k % 2), 8), k // 2, peer],
                dst_ref=arecv.at[k, q],
                send_sem=a_send.at[k],
                recv_sem=a_recv.at[k],
                device_id=(peer * 2 + core, n),
                device_id_type=MESH,
            ).start()

    give_modes = pltpu.make_async_remote_copy(
        src_ref=modv.at[core], dst_ref=modv.at[core], send_sem=t_sem.at[2],
        recv_sem=t_sem.at[3], device_id=(sib, n), device_id_type=MESH,
    )
    give_modes.start()
    give_table = pltpu.make_async_remote_copy(
        src_ref=table, dst_ref=tabv.at[core], send_sem=t_sem.at[4],
        recv_sem=t_sem.at[5], device_id=(sib, n), device_id_type=MESH,
    )
    send_field(0)
    give_table.start()
    send_field(1)

    inv_in.wait()
    arrive = lax.broadcasted_iota(jnp.int32, (512, 512), 0)
    natural = (
        ((arrive // 8) % 16) * 32 + (arrive // 256) * 16 + ((arrive // 128) % 2) * 8 + arrive % 8
    )
    radius = lax.broadcasted_iota(jnp.int32, (512, 512), 1)
    perm[...] = jnp.where(radius == natural, 1.0, 0.0).astype(BF16)

    def reorder(t, carry):
        invo[t] = lax.dot_general(
            perm[...], invv[t], (((1,), (1,)), ((), ())), preferred_element_type=F32
        ).astype(BF16)
        return carry

    lax.fori_loop(0, 8, reorder, 0)
    inv_out = pltpu.make_async_copy(invo, invt, i_sem.at[1])
    inv_out.start()

    own_table.wait()
    give_modes.wait()
    give_table.wait()

    right, opposite, left = (lax.rem(n + d, NARROW) for d in range(1, NARROW))

    def landed(ref, sem):
        pltpu.make_async_copy(ref, ref, sem).wait()

    def hop(src, dst, to, send_sem, recv_sem):
        pltpu.make_async_remote_copy(
            src_ref=src, dst_ref=dst, send_sem=send_sem, recv_sem=recv_sem,
            device_id=(w, to), device_id_type=MESH,
        ).start()

    def transform(k):
        landed(arecv.at[k], a_recv.at[k])
        if k + 2 < NCH:
            send_field(k + 2)

        def turn(t, carry):
            block = arecv[k, pl.ds(2 * t, 2)].reshape(16, 16, TB)
            ft[:, pl.ds(pl.multiple_of(16 * t, 16), 16), :] = jnp.swapaxes(block, 0, 1)
            return carry

        lax.fori_loop(0, 8, turn, 0)

        def two_pairs(pp, carry):
            side = pp // 2
            first = 2 * (pp % 2)
            for e in range(2):
                for kind in range(2):
                    slot = first + e + 4 * kind
                    res[e, kind] = lax.dot_general(
                        tabv[side, slot], ft[side * 8 + slot],
                        (((1,), (1,)), ((), ())), preferred_element_type=F32,
                    )

            at32 = lax.broadcasted_iota(jnp.int32, (32, 128), 0)

            def part(e, kind, block):
                rows = res[e, kind, pl.ds(pl.multiple_of(block * 32, 32), 32), :]
                m = modv[side, pl.ds(first + e + 4 * kind, 1), :]
                return jnp.where(at32 + block * 32 >= m, rows, 0.0)

            def put(pos, vals):
                for t in range(NARROW):
                    both = jnp.concatenate([v[8 * t:8 * t + 8] for v in vals], axis=0)
                    pbuf[k, t, pl.ds(pl.multiple_of(pos * 64 + pp * 16, 16), 16), :] = (
                        both.astype(BF16)
                    )

            put(0, [part(e, 1, 31) for e in range(2)])
            put(32, [part(e, 0, 31) for e in range(2)])

            def fold(v, c2):
                put(v + 1, [part(e, 0, v) + part(e, 1, 30 - v) for e in range(2)])
                return c2

            lax.fori_loop(0, 31, fold, 0)
            return carry

        lax.fori_loop(0, 4, two_pairs, 0)
        hop(pbuf.at[k, opposite, pl.ds(0, HALF)], bpass.at[k, 0], right, b_send.at[k, 0], b_recv.at[k, 0])
        hop(pbuf.at[k, opposite, pl.ds(HALF, HALF)], bpass.at[k, 1], left, b_send.at[k, 1], b_recv.at[k, 1])
        hop(pbuf.at[k, right, pl.ds(HALF, HALF)], brecv.at[k, 0, pl.ds(HALF, HALF)], right, b_send.at[k, 2], b_recv.at[k, 2])
        hop(pbuf.at[k, left, pl.ds(0, HALF)], brecv.at[k, 1, pl.ds(0, HALF)], left, b_send.at[k, 3], b_recv.at[k, 3])

    def combine(k):
        for way, (to, base) in enumerate(((right, 0), (left, HALF))):
            landed(bpass.at[k, way], b_recv.at[k, way])

            def add(t, carry):
                here = pl.ds(pl.multiple_of(base + t * 96, 32), 96)
                there = pl.ds(pl.multiple_of(t * 96, 32), 96)
                pbuf[k, to, here, :] = (
                    pbuf[k, to, here, :].astype(F32) + bpass[k, way, there, :].astype(F32)
                ).astype(BF16)
                return carry

            lax.fori_loop(0, HALF // 96, add, 0)
            half = pl.ds(base, HALF)
            hop(pbuf.at[k, to, half], brecv.at[k, way, half], to, b_send.at[k, 4 + way], b_recv.at[k, 4 + way])

    def spectral(k):
        landed(brecv.at[k, 0, pl.ds(HALF, HALF)], b_recv.at[k, 2])
        landed(brecv.at[k, 1, pl.ds(0, HALF)], b_recv.at[k, 3])
        landed(brecv.at[k, 0, pl.ds(0, HALF)], b_recv.at[k, 4])
        landed(brecv.at[k, 1, pl.ds(HALF, HALF)], b_recv.at[k, 5])

        def modes_of(kind):
            return jnp.concatenate(
                [modv[s, 4 * kind:4 * kind + 4, :] for s in range(2)], axis=0
            )

        lo_modes, hi_modes = modes_of(0), modes_of(1)
        at = lax.broadcasted_iota(jnp.int32, (8, 8, 128), 0)

        upper = lax.broadcasted_iota(jnp.int32, (8, 8, 128), 1) < 4

        def total(pos, v, m):
            rows = pl.ds(pl.multiple_of(pos * 64, 64), 64)
            vals = pbuf[k, n, rows, :].astype(F32)
            for d in range(2):
                vals = vals + brecv[k, d, rows, :].astype(F32)
            turned = jnp.swapaxes(vals.reshape(8, 8, 128), 0, 1)
            return jnp.where(at + (v * 32 + n * 8) >= m[None], turned, 0.0)

        def low(v, carry):
            lo = total(v + 1, v, lo_modes).reshape(4, 16, 128)
            csend[k, v, :, pl.ds(0, 16), :] = lo.astype(BF16)
            return carry

        def high(v, carry):
            lo = total(v + 1, v, lo_modes)
            hi = total(31 - v, v, hi_modes)
            first = jnp.where(upper, lo, pltpu.roll(hi, 4, 1))
            second = jnp.where(upper, pltpu.roll(lo, 4, 1), hi)
            both = jnp.concatenate([first, second], axis=1).reshape(4, 32, 128)
            csend[k, v] = both.astype(BF16)
            return carry

        lax.fori_loop(0, WIDE // 2, low, 0)
        lax.fori_loop(WIDE // 2, WIDE, high, 0)

        target = crecv.at[:, k, q, core]

        def keep(count):
            pltpu.make_async_copy(
                csend.at[k, w, :, pl.ds(0, count)], target.at[:, pl.ds(0, count)], c_recv.at[k]
            ).start()

        @pl.when(w >= WIDE // 2)
        def _():
            keep(32)

        @pl.when(w < WIDE // 2)
        def _():
            keep(16)

        def give(t, carry):
            u = lax.rem(t, 16)
            to = (
                16 - 16 * (t // 16) + 8 * lax.rem(y + u, 2) + 2 * lax.rem(z + u // 2, 4)
                + lax.rem(core + u // 8, 2)
            )

            def go(count):
                pltpu.make_async_remote_copy(
                    src_ref=csend.at[k, to, :, pl.ds(0, count)],
                    dst_ref=target.at[:, pl.ds(0, count)],
                    send_sem=c_send.at[k], recv_sem=c_recv.at[k],
                    device_id=(to, n), device_id_type=MESH,
                ).start()

            @pl.when((to >= WIDE // 2) & (to != w))
            def _():
                go(32)

            @pl.when((to < WIDE // 2) & (to != w))
            def _():
                go(16)

            return carry

        lax.fori_loop(0, WIDE, give, 0)

    def received(k):
        @pl.when(w >= WIDE // 2)
        def _():
            landed(crecv.at[:, k], c_recv.at[k])

        @pl.when(w < WIDE // 2)
        def _():
            landed(crecv.at[:, k, :, :, pl.ds(0, 16)], c_recv.at[k])

    for k in range(NCH):
        transform(k)
        if k:
            spectral(k - 1)
        combine(k)
    spectral(NCH - 1)
    for k in range(NCH):
        received(k)

    for k in range(NCH):
        landed(arecv.at[k, pl.ds(0, 15)], a_send.at[k])
        for i in range(6):
            landed(bpass.at[k, 0], b_send.at[k, i])

        @pl.when(w >= WIDE // 2)
        def _():
            landed(csend.at[k, pl.ds(0, 23)], c_send.at[k])

        @pl.when(w < WIDE // 2)
        def _():
            landed(csend.at[k, pl.ds(0, 23)], c_send.at[k])
            landed(csend.at[k, 0, :, pl.ds(0, 16)], c_send.at[k])
    inv_out.wait()


def solve_upper(x, inv, pair, e):
    blocks = [
        jnp.concatenate(
            [
                x[pair, 2 * c + g, :, half, 16 * e:16 * e + 16, :].reshape(CHIPS * 16, 128)
                for c in range(2)
            ],
            axis=0,
        )
        for half in range(2) for g in range(2)
    ]
    got = jnp.dot(
        jnp.concatenate(blocks, axis=1), inv[2 * pair + e], preferred_element_type=F32
    )
    return got.reshape(2, 256, 512)


def solve_lower(x, inv, pair, e):
    blocks = []
    for half in range(2):
        for g in range(2):
            both = []
            for c in range(2):
                two = x[pair, 2 * c + g, :, half, 0:16, :].astype(F32)
                both.append(two[:, 8 * e:8 * e + 8].reshape(CHIPS * 8, 128).astype(BF16))
            blocks.append(jnp.concatenate(both, axis=0))
    got = jnp.dot(
        jnp.concatenate(blocks, axis=1), inv[2 * pair + e], preferred_element_type=F32
    ).reshape(2 * CHIPS, 8, 512)
    upper = lax.broadcasted_iota(jnp.int32, (2 * CHIPS, 8, 512), 1) < 4
    first = jnp.where(upper, got, 0.0)
    second = jnp.where(upper, pltpu.roll(got, 4, 1), 0.0)
    return jnp.concatenate([first, second], axis=1).reshape(2, 256, 512)


def solve_kernel(where, x, inv, solved, xv, invv, outv, x_sem, i_sem, o_sem):
    def run(rows, solve):
        def rows_of(pair):
            part = (pair, slice(None), slice(None), slice(None), pl.ds(0, rows))
            return pltpu.make_async_copy(x.at[part], xv.at[part], x_sem.at[pair])

        def inverse_of(t):
            return pltpu.make_async_copy(inv.at[t], invv.at[t], i_sem.at[t])

        def fetch(pair, carry):
            rows_of(pair).start()
            inverse_of(2 * pair).start()
            inverse_of(2 * pair + 1).start()
            return carry

        lax.fori_loop(0, 4, fetch, 0)

        def degrees(pair, carry):
            rows_of(pair).wait()
            for e in range(2):
                t = 2 * pair + e
                inverse_of(t).wait()
                outv[t] = solve(xv, invv, pair, e)
                for c in range(2):
                    pltpu.make_async_copy(outv.at[t, c], solved.at[t, c], o_sem).start()
            return carry

        lax.fori_loop(0, 4, degrees, 0)

    @pl.when(where[0] >= WIDE // 2)
    def _():
        run(32, solve_upper)

    @pl.when(where[0] < WIDE // 2)
    def _():
        run(16, solve_lower)

    pltpu.make_async_copy(outv, outv, o_sem).wait()


def per_device(field, table, inverse, modes):
    fields = field.reshape(16, 2, CHIPS, 16, TB)
    any_spec = pl.BlockSpec(memory_space=pl.ANY)
    dma = pltpu.SemaphoreType.DMA
    crecv, invt = pl.pallas_call(
        transform_kernel,
        name="transform",
        out_shape=(
            jax.ShapeDtypeStruct((4, NCH, CHIPS, 2, 32, 128), BF16),
            jax.ShapeDtypeStruct((8, 512, 512), BF16),
        ),
        in_specs=[any_spec, any_spec, pl.BlockSpec(memory_space=pltpu.SMEM), any_spec],
        out_specs=(any_spec, any_spec),
        scratch_shapes=[
            pltpu.VMEM((NCH, CHIPS, 8, 16, TB), BF16),
            pltpu.VMEM((2, 8, DEG, TB), BF16),
            pltpu.VMEM((2, 8, 128), jnp.int32),
            pltpu.VMEM((16, 128, TB), BF16),
            pltpu.VMEM((2, 2, DEG, 128), F32),
            pltpu.VMEM((NCH, NARROW, ROWS, 128), BF16),
            pltpu.VMEM((NCH, 2, ROWS, 128), BF16),
            pltpu.VMEM((NCH, 2, HALF, 128), BF16),
            pltpu.VMEM((NCH, WIDE, 4, 32, 128), BF16),
            pltpu.VMEM((8, 512, 512), BF16),
            pltpu.VMEM((8, 512, 512), BF16),
            pltpu.VMEM((512, 512), BF16),
            dma((NCH,)), dma((NCH,)), dma((6,)), dma((NCH, 6)), dma((NCH, 6)),
            dma((NCH,)), dma((NCH,)), dma((2,)),
        ],
        compiler_params=pltpu.CompilerParams(
            collective_id=0, has_side_effects=True, vmem_limit_bytes=60 * 2**20
        ),
    )(fields, table, modes, inverse)
    where = lax.axis_index("wide").astype(jnp.int32).reshape(1)
    return pl.pallas_call(
        solve_kernel,
        name="solve",
        out_shape=jax.ShapeDtypeStruct((8, 2, 256, 512), F32),
        in_specs=[pl.BlockSpec(memory_space=pltpu.SMEM), any_spec, any_spec],
        out_specs=any_spec,
        scratch_shapes=[
            pltpu.VMEM((4, NCH, CHIPS, 2, 32, 128), BF16),
            pltpu.VMEM((8, 512, 512), BF16),
            pltpu.VMEM((8, 2, 256, 512), F32),
            dma((4,)), dma((8,)), dma(()),
        ],
        compiler_params=pltpu.CompilerParams(vmem_limit_bytes=60 * 2**20),
    )(where, crecv, invt)


def solution(mesh):
    placed = (
        P("wide", None, None, "narrow"),
        P("wide", None, "narrow"),
        P(("wide", "narrow"), None, None),
        P("wide"),
    )
    return jax.shard_map(
        per_device,
        mesh=mesh,
        in_specs=placed,
        out_specs=P(("wide", "narrow"), None, None, None),
        check_vma=False,
    )
```
